512 devices in a mesh: slab: 32 (over z, core), row: 16 (over y, x).
Axes of the slice: x: 4, y: 4, z: 16, core: 2. Of those that a mesh axis runs over, the one named last changes fastest.
Arguments:
- schur_own: float32 [32, 8192, 768], P('slab', 'row'), may hold values from -16 to 16, as said below
- outgoing: float32 [32, 8192, 768], P('slab', 'row'), may hold values from -12 to 12, as said below
Outputs:
- factor: float32 [32, 8192, 512], P('slab', 'row')
- trailing: float32 [32, 8192, 256], P('slab', 'row')
The draws below stay inside these ranges and needn't reach their ends.
Inputs may be any that keep to these rules, and one draw needn't show every extreme that they name: On every slab s, rows 0 .. 767 of schur_own[s] are symmetric, and so are those of outgoing[s]; schur_own[s] minus previous[s] there is positive definite (for slab 0, schur_own[0] itself). `outgoing`: rows 0 .. 767 of each slab are symmetric.
All inputs are finite; a program needn't handle non-finite values.
Results may differ from the reference program's by a relative error of at most 0.0001.
Values sent between devices are 32-bit elements; how exact they have to be, the bound alone decides.
No kernel may reach another device: no remote copies, remote signals or barrier semaphores. Data moves between devices by JAX's collectives and lax.ppermute only.
A program may use at most 64 MiB of HBM per device.

```python
import math
import jax
import jax.numpy as jnp
from jax import lax

W = 8192
NB = 256
PANELS = 2
PANELW = 512
COLS = 768
SLABS = 32


def block_draw(key, diag_low, diag_high, off_scale, tall_scale, kernel_amp):
    first_key, second_key = jax.random.split(key, 2)
    raw_draw = jnp.clip(jax.random.normal(first_key, (SLABS, W, COLS), jnp.float32), -4.0, 4.0)
    upper_rows = raw_draw[:, :COLS, :]
    symmetric = (upper_rows + jnp.swapaxes(upper_rows, 1, 2)) * (off_scale / math.sqrt(2.0 * COLS))
    identity = jnp.eye(COLS, dtype=jnp.float32)
    diagonal = jax.random.uniform(second_key, (SLABS, COLS, 1), jnp.float32, diag_low, diag_high)
    upper_rows = symmetric * (1.0 - identity) + diagonal * identity
    positions = jnp.arange(COLS).astype(jnp.float32)
    distance = jnp.abs(positions[:, None] - positions[None, :])
    kernel = kernel_amp * jnp.exp(-distance / (NB / 8.0))
    upper_rows = upper_rows + kernel[None, :, :]
    tall_rows = raw_draw[:, COLS:, :] * tall_scale
    return jnp.concatenate([upper_rows, tall_rows], axis=1)


def draw_schur_own(key, part):
    key = jax.random.fold_in(key, 11)
    return block_draw(key, 3.0, 5.0, 0.7, 1.0, 1.0)


def draw_outgoing(key, part):
    key = jax.random.fold_in(key, 23)
    return block_draw(key, 0.2, 1.0, 0.3, 0.7, 0.0)


def setup_inputs(seed: int = 0) -> dict:
    key_of = jax.random.split(jax.random.key(seed), 3)
    schur_own = draw_schur_own(jax.random.fold_in(key_of[2], 71), 0)
    outgoing = draw_outgoing(jax.random.fold_in(key_of[2], 71), 0)
    return dict(schur_own=schur_own, outgoing=outgoing)


def factor_slab(own_block, previous):
    schur_block = own_block - previous
    head_cols = schur_block[:, :PANELW]
    trail_cols = schur_block[:, PANELW:]
    global_rows = jnp.arange(W)
    identity = jnp.eye(NB, dtype=jnp.float32)
    factors = []
    for panel_index in range(PANELS):
        first_col = panel_index * NB
        panel_cols = head_cols[:, first_col:first_col + NB]
        diag_factor = lax.linalg.cholesky(panel_cols[first_col:first_col + NB])
        inverse = lax.linalg.triangular_solve(diag_factor, identity, left_side=True, lower=True)
        row_mask = (global_rows >= first_col).astype(jnp.float32)[:, None]
        lower_cols = jnp.dot(panel_cols, inverse.T, precision=lax.Precision.HIGHEST) * row_mask
        window = lower_cols[first_col + NB:COLS]
        update = jnp.dot(lower_cols, window.T, precision=lax.Precision.HIGHEST)
        head_left = PANELW - first_col - NB
        head_cols = head_cols.at[:, first_col + NB:].add(-update[:, :head_left])
        trail_cols = trail_cols - update[:, head_left:]
        factors.append(lower_cols)
    trail_mask = (global_rows >= PANELW).astype(jnp.float32)[:, None]
    return (jnp.concatenate(factors, axis=1), trail_cols * trail_mask)

def reference(schur_own, outgoing):
    previous = jnp.concatenate([jnp.zeros_like(outgoing[:1]), outgoing[:-1]], axis=0)
    factor, trailing = lax.map(lambda slab_pair: factor_slab(slab_pair[0], slab_pair[1]), (schur_own, previous))
    return (factor, trailing)
```

```python
import jax
import jax.numpy as jnp
from jax import lax
from jax.experimental import pallas as pl
from jax.experimental.pallas import tpu as pltpu
from jax.sharding import PartitionSpec as P

NB = 256
PANELW = 512
COLS = 768
STRIP = 32
SUB = 8
LANES = 128
VMEM_BYTES = 48 * 1024 * 1024


def dot(a, b, contract):
    return lax.dot_general(
        a, b, ((contract[:1], contract[1:]), ((), ())),
        precision=lax.Precision.HIGHEST, preferred_element_type=jnp.float32,
    )


def eliminate_strip(rows, first):
    groups = len(rows)
    lane = lax.broadcasted_iota(jnp.int32, (SUB, NB), 1)
    sub = lax.broadcasted_iota(jnp.int32, (SUB, NB), 0)
    for t in range(groups):
        col = first + SUB * t
        in_block = (lane >= col) & (lane < col + SUB)
        columns = [
            [jnp.broadcast_to(rows[g][:, col + j : col + j + 1], (SUB, LANES)) for j in range(SUB)]
            for g in range(t, groups)
        ]
        a = [
            [jnp.broadcast_to(columns[0][k][i : i + 1, :], (SUB, LANES)) if i >= k else None
             for k in range(SUB)]
            for i in range(SUB)
        ]
        start = jnp.where(in_block, (lane == col + sub).astype(jnp.float32), rows[t])
        u = [jnp.broadcast_to(start[i : i + 1, :], (SUB, NB)) for i in range(SUB)]
        inv = [None] * SUB
        low = [[None] * SUB for _ in range(SUB)]
        for j in range(SUB):
            inv[j] = lax.rsqrt(a[j][j])
            for k in range(j + 1, SUB):
                low[k][j] = a[k][j] * inv[j]
            for k in range(j + 1, SUB):
                for m in range(j + 1, k + 1):
                    a[k][m] = a[k][m] - low[k][j] * low[m][j]
        wide = lambda x: jnp.concatenate([x, x], axis=1)
        for j in range(SUB):
            u[j] = u[j] * wide(inv[j])
            for k in range(j + 1, SUB):
                u[k] = u[k] - wide(low[k][j]) * u[j]
        packed = u[0]
        for j in range(1, SUB):
            packed = jnp.where(sub == j, u[j], packed)
        rows[t] = packed
        for g in range(t + 1, groups):
            col_g = columns[g - t]
            total = jnp.where(in_block, 0.0, rows[g])
            for j in range(SUB):
                col_g[j] = col_g[j] * inv[j]
                for k in range(j + 1, SUB):
                    col_g[k] = col_g[k] - col_g[j] * low[k][j]
                total = total - wide(col_g[j]) * u[j]
            rows[g] = total
    return rows


def invert_factor(work, between=None):
    groups = STRIP // SUB
    for s in range(NB // STRIP):
        first = STRIP * s
        after = first + STRIP
        rows = [work[first + SUB * g : first + SUB * (g + 1), :] for g in range(groups)]
        rows = eliminate_strip(rows, first)
        strip = jnp.concatenate(rows, axis=0)
        lane = lax.broadcasted_iota(jnp.int32, (STRIP, NB), 1)
        row = lax.broadcasted_iota(jnp.int32, (STRIP, NB), 0) + first
        strip = jnp.where((lane > row) & (lane < after), 0.0, strip)
        work[first:after, :] = jnp.where(lane < after, strip, 0.0)
        if between is not None:
            between(s)
        if after < NB:
            base = after // LANES * LANES
            update = dot(strip[:, base:], strip, (0, 0))[after - base :, :]
            lane = lax.broadcasted_iota(jnp.int32, (NB - after, NB), 1)
            below = jnp.where((lane >= first) & (lane < after), 0.0, work[after:, :])
            work[after:, :] = below - update


def first_kernel(block, inverse):
    inverse[...] = block[...]
    invert_factor(inverse)


def second_kernel(row_index, inverse0, head, own, prev, factor, trailing, work, middle, tail):
    x0 = inverse0[...]
    w1 = dot(x0, head[:NB, :NB], (1, 0))
    w2 = dot(x0, head[:NB, NB:], (1, 0))
    work[...] = head[NB:, :NB] - dot(w1, w1, (0, 0))
    cross = head[NB:, NB:] - dot(w1, w2, (0, 0))
    rows_here = own.shape[0]
    piece = rows_here // (NB // STRIP)

    def between(s):
        at = pl.ds(s * piece, piece)
        lower = dot(own[at, :NB] - prev[at, :NB], x0, (1, 1))
        factor[at, :NB] = lower
        middle[at, :] = own[at, NB:PANELW] - prev[at, NB:PANELW] - dot(lower, w1, (1, 0))
        tail[at, :] = own[at, PANELW:] - prev[at, PANELW:] - dot(lower, w2, (1, 0))

    invert_factor(work, between)
    x1 = work[...]
    w3 = dot(x1, cross, (1, 0))
    first_row = row_index[0] * rows_here
    row = first_row + lax.broadcasted_iota(jnp.int32, (rows_here, NB), 0)
    lower = jnp.where(row >= NB, dot(middle[...], x1, (1, 1)), 0.0)
    factor[:, NB:] = lower
    trailing[...] = jnp.where(row >= PANELW, tail[...] - dot(lower, w3, (1, 0)), 0.0)


def spread(block):
    return lax.all_to_all(block, "row", 0, 0, tiled=True)[0]


def gather(chunk):
    count = lax.axis_size("row")
    sent = jnp.broadcast_to(chunk[None], (count,) + chunk.shape)
    full = lax.all_to_all(sent, "row", 0, 0, tiled=True)
    return full.reshape((-1, chunk.shape[1]))


def per_device(schur_own, outgoing):
    own = schur_own[0]
    out = outgoing[0]
    count = lax.axis_size("row")
    slabs = lax.axis_size("slab")
    pairs = [(s, s + 1) for s in range(slabs - 1)]
    vmem = pl.BlockSpec(memory_space=pltpu.VMEM)
    params = pltpu.CompilerParams(vmem_limit_bytes=VMEM_BYTES)

    part = NB // count
    both = jnp.concatenate(
        [x[:NB, :NB].reshape(count, part, NB) for x in (own, out)], axis=1
    )
    shared = spread(both)
    chunk = shared[:part] - lax.ppermute(shared[part:], "slab", pairs)
    prev_right = lax.ppermute(out[:, NB:], "slab", pairs)
    first = gather(chunk)
    inverse0 = pl.pallas_call(
        first_kernel,
        out_shape=jax.ShapeDtypeStruct((NB, NB), jnp.float32),
        in_specs=[vmem], out_specs=vmem, compiler_params=params,
        cost_estimate=pl.CostEstimate(flops=6 * NB**3, bytes_accessed=8 * NB**2, transcendentals=NB),
        name="panel_inverse",
    )(first)
    head_chunk = spread((own[:, NB:] - prev_right).reshape(count, -1, COLS - NB))
    head = gather(head_chunk)
    prev_left = lax.ppermute(out[:, :NB], "slab", pairs)
    prev = jnp.concatenate([prev_left, prev_right], axis=1)
    rows_here = own.shape[0]
    factor, trailing = pl.pallas_call(
        second_kernel,
        out_shape=(
            jax.ShapeDtypeStruct((rows_here, PANELW), jnp.float32),
            jax.ShapeDtypeStruct((rows_here, COLS - PANELW), jnp.float32),
        ),
        in_specs=[pl.BlockSpec(memory_space=pltpu.SMEM)] + [vmem] * 4,
        out_specs=(vmem, vmem),
        scratch_shapes=[
            pltpu.VMEM((NB, NB), jnp.float32),
            pltpu.VMEM((rows_here, NB), jnp.float32),
            pltpu.VMEM((rows_here, NB), jnp.float32),
        ],
        compiler_params=params,
        name="panel_update",
    )(lax.axis_index("row").astype(jnp.int32)[None], inverse0, head, own, prev)
    return factor[None], trailing[None]


def solution(mesh):
    specs = (P("slab", "row", None), P("slab", "row", None))
    return jax.shard_map(
        per_device, mesh=mesh, in_specs=specs, out_specs=specs, check_vma=False
    )
```

```python
import functools

import jax
import jax.numpy as jnp
from jax import lax
from jax.experimental import pallas as pl
from jax.experimental.pallas import tpu as pltpu
from jax.sharding import Mesh, PartitionSpec as P

NB = 256
PANELW = 512
COLS = 768
ROWS_Y = 4
STRIP = 32
SUB = 8
LANES = 128
VMEM_BYTES = 48 * 1024 * 1024


def dot(a, b, contract):
    return lax.dot_general(
        a, b, ((contract[:1], contract[1:]), ((), ())),
        precision=lax.Precision.HIGHEST, preferred_element_type=jnp.float32,
    )


def eliminate_strip(rows, first):
    groups = len(rows)
    lane = lax.broadcasted_iota(jnp.int32, (SUB, NB), 1)
    sub = lax.broadcasted_iota(jnp.int32, (SUB, NB), 0)
    for t in range(groups):
        col = first + SUB * t
        in_block = (lane >= col) & (lane < col + SUB)
        columns = [
            [jnp.broadcast_to(rows[g][:, col + j : col + j + 1], (SUB, LANES)) for j in range(SUB)]
            for g in range(t, groups)
        ]
        a = [
            [jnp.broadcast_to(columns[0][k][i : i + 1, :], (SUB, LANES)) if i >= k else None
             for k in range(SUB)]
            for i in range(SUB)
        ]
        start = jnp.where(in_block, (lane == col + sub).astype(jnp.float32), rows[t])
        u = [jnp.broadcast_to(start[i : i + 1, :], (SUB, NB)) for i in range(SUB)]
        inv = [None] * SUB
        low = [[None] * SUB for _ in range(SUB)]
        for j in range(SUB):
            inv[j] = lax.rsqrt(a[j][j])
            for k in range(j + 1, SUB):
                low[k][j] = a[k][j] * inv[j]
            for k in range(j + 1, SUB):
                for m in range(j + 1, k + 1):
                    a[k][m] = a[k][m] - low[k][j] * low[m][j]
        wide = lambda x: jnp.concatenate([x, x], axis=1)
        for j in range(SUB):
            u[j] = u[j] * wide(inv[j])
            for k in range(j + 1, SUB):
                u[k] = u[k] - wide(low[k][j]) * u[j]
        packed = u[0]
        for j in range(1, SUB):
            packed = jnp.where(sub == j, u[j], packed)
        rows[t] = packed
        for g in range(t + 1, groups):
            col_g = columns[g - t]
            total = jnp.where(in_block, 0.0, rows[g])
            for j in range(SUB):
                col_g[j] = col_g[j] * inv[j]
                for k in range(j + 1, SUB):
                    col_g[k] = col_g[k] - col_g[j] * low[k][j]
                total = total - wide(col_g[j]) * u[j]
            rows[g] = total
    return rows


def invert_factor(work, strips=range(NB // STRIP), between=None):
    groups = STRIP // SUB
    for s in strips:
        first = STRIP * s
        after = first + STRIP
        rows = [work[first + SUB * g : first + SUB * (g + 1), :] for g in range(groups)]
        rows = eliminate_strip(rows, first)
        strip = jnp.concatenate(rows, axis=0)
        lane = lax.broadcasted_iota(jnp.int32, (STRIP, NB), 1)
        row = lax.broadcasted_iota(jnp.int32, (STRIP, NB), 0) + first
        strip = jnp.where((lane > row) & (lane < after), 0.0, strip)
        work[first:after, :] = jnp.where(lane < after, strip, 0.0)
        if between is not None:
            between(s)
        if after < NB:
            base = after // LANES * LANES
            update = dot(strip[:, base:], strip, (0, 0))[after - base :, :]
            lane = lax.broadcasted_iota(jnp.int32, (NB - after, NB), 1)
            below = jnp.where((lane >= first) & (lane < after), 0.0, work[after:, :])
            work[after:, :] = below - update


def first_kernel(strips, block, inverse):
    inverse[...] = block[...]
    invert_factor(inverse, strips)


def second_kernel(row_index, inverse0, head, own, prev, factor, trailing, work, middle, tail):
    x0 = inverse0[...]
    half = head.shape[0] // 2
    pick = lambda at, source: head[pl.ds(at, half), source].reshape((NB, NB))
    w1 = dot(x0, pick(0, 0), (1, 0))
    w2 = dot(x0, pick(0, 1), (1, 1))
    work[...] = pick(half, 0) - dot(w1, w1, (0, 0))
    cross = pick(half, 1) - dot(w2, w1, (0, 0))
    rows_here = own.shape[0]
    piece = rows_here // (NB // STRIP)

    def between(s):
        at = pl.ds(s * piece, piece)
        lower = dot(own[at, :NB] - prev[at, :NB], x0, (1, 1))
        factor[at, :NB] = lower
        middle[at, :] = own[at, NB:PANELW] - prev[at, NB:PANELW] - dot(lower, w1, (1, 0))
        tail[at, :] = own[at, PANELW:] - prev[at, PANELW:] - dot(lower, w2, (1, 0))

    invert_factor(work, between=between)
    x1 = work[...]
    w3 = dot(x1, cross, (1, 1))
    first_row = row_index[0] * rows_here
    row = first_row + lax.broadcasted_iota(jnp.int32, (rows_here, NB), 0)
    lower = jnp.where(row >= NB, dot(middle[...], x1, (1, 1)), 0.0)
    factor[:, NB:] = lower
    trailing[...] = jnp.where(row >= PANELW, tail[...] - dot(lower, w3, (1, 0)), 0.0)


def exchange(blocks, axis):
    return lax.all_to_all(blocks, axis, 0, 0, tiled=True)


def copies(chunk, axis):
    return jnp.broadcast_to(chunk[None], (lax.axis_size(axis),) + chunk.shape)


def per_device(schur_own, outgoing):
    own = schur_own[0]
    out = outgoing[0]
    rows_here = own.shape[0]
    across = lax.axis_size("x")
    plane = lax.axis_size("y") * across
    row_index = lax.axis_index("y") * across + lax.axis_index("x")
    pairs = [(s, s + 1) for s in range(lax.axis_size("slab") - 1)]
    vmem = pl.BlockSpec(memory_space=pltpu.VMEM)
    params = pltpu.CompilerParams(vmem_limit_bytes=VMEM_BYTES)

    def inverse_step(block, strips, name):
        return pl.pallas_call(
            functools.partial(first_kernel, strips),
            out_shape=jax.ShapeDtypeStruct((NB, NB), jnp.float32),
            in_specs=[vmem], out_specs=vmem, compiler_params=params,
            cost_estimate=pl.CostEstimate(
                flops=3 * NB**3, bytes_accessed=8 * NB**2, transcendentals=NB),
            name=name,
        )(block)

    corner = own[:NB, :NB] - lax.ppermute(out[:NB, :NB], "slab", pairs)
    prev = lax.ppermute(out, "slab", pairs)
    part = exchange(corner.reshape(across, -1, NB), "x")[0]
    part = exchange(copies(part, "y"), "y")[0]
    first = exchange(copies(part, "x"), "x").reshape(NB, NB)

    head = own[:, NB:PANELW] - prev[:, NB:PANELW]
    side = own[:NB, :PANELW] - prev[:NB, :PANELW]
    side = jnp.concatenate([side[:, :NB], side[:, NB:]], axis=0)
    mine = jnp.where(row_index == 1, side, head)
    mine, first = lax.optimization_barrier((mine, first))
    shared = exchange(mine.reshape(plane, -1, NB), ("y", "x"))[:2]
    start = inverse_step(first, range(0, 4), "inverse_left")
    shared, start = lax.optimization_barrier((shared, start))
    shared = exchange(copies(shared, ("y", "x")), ("y", "x"))
    inverse0 = inverse_step(start, range(4, 8), "inverse_right")

    factor, trailing = pl.pallas_call(
        second_kernel,
        out_shape=(
            jax.ShapeDtypeStruct((rows_here, PANELW), jnp.float32),
            jax.ShapeDtypeStruct((rows_here, COLS - PANELW), jnp.float32),
        ),
        in_specs=[pl.BlockSpec(memory_space=pltpu.SMEM)] + [vmem] * 4,
        out_specs=(vmem, vmem),
        scratch_shapes=[
            pltpu.VMEM((NB, NB), jnp.float32),
            pltpu.VMEM((rows_here, NB), jnp.float32),
            pltpu.VMEM((rows_here, NB), jnp.float32),
        ],
        compiler_params=params,
        name="panel_update",
    )(row_index.astype(jnp.int32)[None], inverse0, shared, own, prev)
    return factor[None], trailing[None]


def solution(mesh):
    planes = Mesh(mesh.devices.reshape(mesh.shape["slab"], ROWS_Y, -1), ("slab", "y", "x"))
    specs = (P("slab", ("y", "x"), None), P("slab", ("y", "x"), None))
    return jax.shard_map(
        per_device, mesh=planes, in_specs=specs, out_specs=specs, check_vma=False
    )
```

```python
import jax
import jax.numpy as jnp
from jax import lax
from jax.experimental import pallas as pl
from jax.experimental.pallas import tpu as pltpu
from jax.sharding import PartitionSpec as P

NB = 256
PANELW = 512
COLS = 768
ACROSS = 4
STRIP = 32
SUB = 8
LANES = 128
VMEM_BYTES = 48 * 1024 * 1024


def dot(a, b, contract):
    return lax.dot_general(
        a, b, ((contract[:1], contract[1:]), ((), ())),
        precision=lax.Precision.HIGHEST, preferred_element_type=jnp.float32,
    )


def eliminate_strip(rows, first):
    groups = len(rows)
    lane = lax.broadcasted_iota(jnp.int32, (SUB, NB), 1)
    sub = lax.broadcasted_iota(jnp.int32, (SUB, NB), 0)
    for t in range(groups):
        col = first + SUB * t
        in_block = (lane >= col) & (lane < col + SUB)
        columns = [
            [jnp.broadcast_to(rows[g][:, col + j : col + j + 1], (SUB, LANES)) for j in range(SUB)]
            for g in range(t, groups)
        ]
        a = [
            [jnp.broadcast_to(columns[0][k][i : i + 1, :], (SUB, LANES)) if i >= k else None
             for k in range(SUB)]
            for i in range(SUB)
        ]
        start = jnp.where(in_block, (lane == col + sub).astype(jnp.float32), rows[t])
        u = [jnp.broadcast_to(start[i : i + 1, :], (SUB, NB)) for i in range(SUB)]
        inv = [None] * SUB
        low = [[None] * SUB for _ in range(SUB)]
        for j in range(0, SUB, 2):
            p, q = a[j][j], a[j + 1][j]
            det = p * a[j + 1][j + 1] - q * q
            inv[j] = lax.rsqrt(p)
            inv[j + 1] = (p * inv[j]) * lax.rsqrt(det)
            for k in range(j + 1, SUB):
                low[k][j] = a[k][j] * inv[j]
            for k in range(j + 2, SUB):
                low[k][j + 1] = (a[k][j + 1] - low[k][j] * low[j + 1][j]) * inv[j + 1]
                for m in range(j + 2, k + 1):
                    a[k][m] = a[k][m] - low[k][j] * low[m][j]
                    a[k][m] = a[k][m] - low[k][j + 1] * low[m][j + 1]
        wide = lambda x: jnp.concatenate([x, x], axis=1)
        for j in range(SUB):
            u[j] = u[j] * wide(inv[j])
            for k in range(j + 1, SUB):
                u[k] = u[k] - wide(low[k][j]) * u[j]
        packed = u[0]
        for j in range(1, SUB):
            packed = jnp.where(sub == j, u[j], packed)
        rows[t] = packed
        for g in range(t + 1, groups):
            col_g = columns[g - t]
            total = jnp.where(in_block, 0.0, rows[g])
            for j in range(SUB):
                col_g[j] = col_g[j] * inv[j]
                for k in range(j + 1, SUB):
                    col_g[k] = col_g[k] - col_g[j] * low[k][j]
                total = total - wide(col_g[j]) * u[j]
            rows[g] = total
    return rows


def thirds(x):
    high = x.astype(jnp.bfloat16)
    rest = x - high.astype(jnp.float32)
    middle = rest.astype(jnp.bfloat16)
    return high, middle, (rest - middle.astype(jnp.float32)).astype(jnp.bfloat16)


def gram(parts, columns):
    high, middle, low = parts
    left = jnp.concatenate([x[:, columns] for x in (high, high, middle, high, low, middle)], axis=0)
    right = jnp.concatenate([high, middle, high, low, high, middle], axis=0)
    return lax.dot_general(
        left, right, (((0,), (0,)), ((), ())), preferred_element_type=jnp.float32
    )


def invert_factor(work, between=None):
    groups = STRIP // SUB
    for half in range(NB // LANES):
        top = half * LANES
        columns = slice(top, top + LANES)
        strips = []
        for s in range(LANES // STRIP):
            first = top + STRIP * s
            after = first + STRIP
            rows = [work[first + SUB * g : first + SUB * (g + 1), :] for g in range(groups)]
            rows = eliminate_strip(rows, first)
            strip = jnp.concatenate(rows, axis=0)
            lane = lax.broadcasted_iota(jnp.int32, (STRIP, NB), 1)
            row = lax.broadcasted_iota(jnp.int32, (STRIP, NB), 0) + first
            strip = jnp.where((lane > row) & (lane < after), 0.0, strip)
            work[first:after, :] = jnp.where(lane < after, strip, 0.0)
            end = top + LANES
            if after < end:
                update = gram(thirds(strip), columns)[after - top :, :]
                lane = lax.broadcasted_iota(jnp.int32, (end - after, NB), 1)
                below = jnp.where((lane >= first) & (lane < after), 0.0, work[after:end, :])
                work[after:end, :] = below - update
            if between is not None:
                between(first // STRIP)
            strips.append(strip)
        if top + LANES < NB:
            upper = jnp.concatenate(strips, axis=0)
            lane = lax.broadcasted_iota(jnp.int32, (LANES, NB), 1)
            row = lax.broadcasted_iota(jnp.int32, (LANES, NB), 0) + top
            upper = jnp.where((lane > row) & (lane < top + LANES), 0.0, upper)
            update = gram(thirds(upper), slice(top + LANES, top + 2 * LANES))
            below = jnp.where(lane < top + LANES, 0.0, work[top + LANES :, :])
            work[top + LANES :, :] = below - update


def pack_kernel(own, prev, packed):
    value = own[...] - prev[...]
    strip_row = lax.broadcasted_iota(jnp.int32, (LANES, LANES), 0) // STRIP
    strip_col = lax.broadcasted_iota(jnp.int32, (LANES, LANES), 1) // STRIP
    packed[:LANES, :] = jnp.where(strip_row <= strip_col, value[:LANES, :LANES], value[LANES:, LANES:])
    packed[LANES : 2 * LANES, :] = value[:LANES, LANES:]
    strip = lax.broadcasted_iota(jnp.int32, (STRIP, LANES), 1) // STRIP
    diagonal = jnp.zeros((STRIP, LANES), jnp.float32)
    for i in range(LANES // STRIP):
        rows = value[LANES + STRIP * i : LANES + STRIP * (i + 1), LANES:]
        diagonal = jnp.where(strip == i, rows, diagonal)
    packed[2 * LANES :, :] = diagonal


def first_kernel(row_index, kept, one, two, three, inverse):
    packed = jnp.where(row_index[0] < ACROSS, kept[...], one[...] + two[...] + three[...])
    strip_row = lax.broadcasted_iota(jnp.int32, (LANES, LANES), 0) // STRIP
    strip_col = lax.broadcasted_iota(jnp.int32, (LANES, LANES), 1) // STRIP
    mixed = packed[:LANES, :]
    diagonal = jnp.concatenate([packed[2 * LANES :, :]] * (LANES // STRIP), axis=0)
    inverse[:LANES, :LANES] = mixed
    inverse[:LANES, LANES:] = packed[LANES : 2 * LANES, :]
    inverse[LANES:, :LANES] = jnp.zeros((LANES, LANES), jnp.float32)
    inverse[LANES:, LANES:] = jnp.where(strip_row < strip_col, mixed.T, diagonal)
    invert_factor(inverse)


def second_kernel(row_index, inverse0, head, own, prev, factor, trailing, work, middle, tail):
    x0 = inverse0[...]
    half = head.shape[0] // 2
    pick = lambda at, source: head[pl.ds(at, half), source].reshape((NB, NB))
    w1 = dot(x0, pick(0, 0), (1, 0))
    w2 = dot(x0, pick(0, 1), (1, 1))
    work[...] = pick(half, 0) - dot(w1, w1, (0, 0))
    cross = pick(half, 1) - dot(w2, w1, (0, 0))
    rows_here = own.shape[0]
    piece = rows_here // (NB // STRIP)

    def between(s):
        at = pl.ds(s * piece, piece)
        lower = dot(own[at, :NB] - prev[at, :NB], x0, (1, 1))
        factor[at, :NB] = lower
        middle[at, :] = own[at, NB:PANELW] - prev[at, NB:PANELW] - dot(lower, w1, (1, 0))
        tail[at, :] = own[at, PANELW:] - prev[at, PANELW:] - dot(lower, w2, (1, 0))

    invert_factor(work, between=between)
    x1 = work[...]
    w3 = dot(x1, cross, (1, 1))
    first_row = row_index[0] * rows_here
    row = first_row + lax.broadcasted_iota(jnp.int32, (rows_here, NB), 0)
    lower = jnp.where(row >= NB, dot(middle[...], x1, (1, 1)), 0.0)
    factor[:, NB:] = lower
    trailing[...] = jnp.where(row >= PANELW, tail[...] - dot(lower, w3, (1, 0)), 0.0)


def exchange(blocks):
    return lax.all_to_all(blocks, "row", 0, 0, tiled=True)


def head_shares(block, row_index, count):
    side = jnp.concatenate([block[:NB, :NB], block[:NB, NB:PANELW]], axis=0)
    mine = jnp.where(row_index == 1, side, block[:, NB:PANELW])
    return mine.reshape(count, -1, NB)


def per_device(schur_own, outgoing):
    own = schur_own[0]
    out = outgoing[0]
    rows_here = own.shape[0]
    count = lax.axis_size("row")
    row_index = lax.axis_index("row").astype(jnp.int32)
    pairs = [(s, s + 1) for s in range(lax.axis_size("slab") - 1)]
    vmem = pl.BlockSpec(memory_space=pltpu.VMEM)
    smem = pl.BlockSpec(memory_space=pltpu.SMEM)
    params = pltpu.CompilerParams(vmem_limit_bytes=VMEM_BYTES)

    prev_corner = lax.ppermute(out[:NB, :NB], "slab", pairs)
    corner = pl.BlockSpec((NB, NB), lambda i: (0, 0))
    packed_rows = 2 * LANES + STRIP
    packed = pl.pallas_call(
        pack_kernel,
        grid=(1,),
        out_shape=jax.ShapeDtypeStruct((packed_rows, LANES), jnp.float32),
        in_specs=[corner, corner],
        out_specs=pl.BlockSpec((packed_rows, LANES), lambda i: (0, 0)),
        compiler_params=params,
        name="pack_corner",
    )(own, prev_corner)
    sent = [lax.ppermute(packed, "row", [(0, d)]) for d in (2, 1, 3)]
    out_shares, _ = lax.optimization_barrier((head_shares(out, row_index, count), prev_corner))
    prev_shares = lax.ppermute(out_shares, "slab", pairs)
    kept = jnp.where(row_index == 0, packed, sent[0] + sent[1] + sent[2])
    kept, prev_shares = lax.optimization_barrier((kept, prev_shares))
    down = [
        lax.ppermute(kept, "row", [(x, ACROSS * d + x) for x in range(ACROSS)]) for d in (2, 1, 3)
    ]
    shares = exchange(head_shares(own, row_index, count) - prev_shares)[:2]
    *down, shares = lax.optimization_barrier((*down, shares))
    head = exchange(jnp.broadcast_to(shares[None], (count,) + shares.shape))
    out, _ = lax.optimization_barrier((out, kept))
    prev = lax.ppermute(out, "slab", pairs)

    inverse0 = pl.pallas_call(
        first_kernel,
        out_shape=jax.ShapeDtypeStruct((NB, NB), jnp.float32),
        in_specs=[smem] + [vmem] * 4,
        out_specs=vmem,
        compiler_params=params,
        cost_estimate=pl.CostEstimate(
            flops=400 * NB**3, bytes_accessed=8 * NB**2, transcendentals=NB),
        name="panel_inverse",
    )(row_index[None], kept, *down)

    factor, trailing = pl.pallas_call(
        second_kernel,
        out_shape=(
            jax.ShapeDtypeStruct((rows_here, PANELW), jnp.float32),
            jax.ShapeDtypeStruct((rows_here, COLS - PANELW), jnp.float32),
        ),
        in_specs=[smem] + [vmem] * 4,
        out_specs=(vmem, vmem),
        scratch_shapes=[
            pltpu.VMEM((NB, NB), jnp.float32),
            pltpu.VMEM((rows_here, NB), jnp.float32),
            pltpu.VMEM((rows_here, NB), jnp.float32),
        ],
        compiler_params=params,
        name="panel_update",
    )(row_index[None], inverse0, head, own, prev)
    return factor[None], trailing[None]


def solution(mesh):
    specs = (P("slab", "row", None), P("slab", "row", None))
    return jax.shard_map(
        per_device, mesh=mesh, in_specs=specs, out_specs=specs, check_vma=False
    )
```

```python
import jax
import jax.numpy as jnp
from jax import lax
from jax.experimental import pallas as pl
from jax.experimental.pallas import tpu as pltpu
from jax.sharding import PartitionSpec as P

NB = 256
PANELW = 512
COLS = 768
ACROSS = 4
STRIP = 32
SUB = 8
LANES = 128
VMEM_BYTES = 48 * 1024 * 1024


def dot(a, b, contract):
    return lax.dot_general(
        a, b, ((contract[:1], contract[1:]), ((), ())),
        precision=lax.Precision.HIGHEST, preferred_element_type=jnp.float32,
    )


def eliminate_strip(rows, first):
    groups = len(rows)
    lane = lax.broadcasted_iota(jnp.int32, (SUB, NB), 1)
    sub = lax.broadcasted_iota(jnp.int32, (SUB, NB), 0)
    for t in range(groups):
        col = first + SUB * t
        in_block = (lane >= col) & (lane < col + SUB)
        columns = [
            [jnp.broadcast_to(rows[g][:, col + j : col + j + 1], (SUB, LANES)) for j in range(SUB)]
            for g in range(t, groups)
        ]
        a = [
            [jnp.broadcast_to(columns[0][k][i : i + 1, :], (SUB, LANES)) if i >= k else None
             for k in range(SUB)]
            for i in range(SUB)
        ]
        start = jnp.where(in_block, (lane == col + sub).astype(jnp.float32), rows[t])
        u = [jnp.broadcast_to(start[i : i + 1, :], (SUB, NB)) for i in range(SUB)]
        inv = [None] * SUB
        low = [[None] * SUB for _ in range(SUB)]
        for j in range(0, SUB, 2):
            p, q = a[j][j], a[j + 1][j]
            det = p * a[j + 1][j + 1] - q * q
            inv[j] = lax.rsqrt(p)
            inv[j + 1] = (p * inv[j]) * lax.rsqrt(det)
            for k in range(j + 1, SUB):
                low[k][j] = a[k][j] * inv[j]
            for k in range(j + 2, SUB):
                low[k][j + 1] = (a[k][j + 1] - low[k][j] * low[j + 1][j]) * inv[j + 1]
                for m in range(j + 2, k + 1):
                    a[k][m] = a[k][m] - low[k][j] * low[m][j]
                    a[k][m] = a[k][m] - low[k][j + 1] * low[m][j + 1]
        wide = lambda x: jnp.concatenate([x, x], axis=1)
        for j in range(SUB):
            u[j] = u[j] * wide(inv[j])
            for k in range(j + 1, SUB):
                u[k] = u[k] - wide(low[k][j]) * u[j]
        packed = u[0]
        for j in range(1, SUB):
            packed = jnp.where(sub == j, u[j], packed)
        rows[t] = packed
        for g in range(t + 1, groups):
            col_g = columns[g - t]
            total = jnp.where(in_block, 0.0, rows[g])
            for j in range(SUB):
                col_g[j] = col_g[j] * inv[j]
                for k in range(j + 1, SUB):
                    col_g[k] = col_g[k] - col_g[j] * low[k][j]
                total = total - wide(col_g[j]) * u[j]
            rows[g] = total
    return rows


def thirds(x):
    high = x.astype(jnp.bfloat16)
    rest = x - high.astype(jnp.float32)
    middle = rest.astype(jnp.bfloat16)
    return high, middle, (rest - middle.astype(jnp.float32)).astype(jnp.bfloat16)


def gram(parts, columns):
    high, middle, low = parts
    left = jnp.concatenate([x[:, columns] for x in (high, high, middle, high, low, middle)], axis=0)
    right = jnp.concatenate([high, middle, high, low, high, middle], axis=0)
    return lax.dot_general(
        left, right, (((0,), (0,)), ((), ())), preferred_element_type=jnp.float32
    )


def invert_factor(work, between=None):
    groups = STRIP // SUB
    for half in range(NB // LANES):
        top = half * LANES
        columns = slice(top, top + LANES)
        strips = []
        for s in range(LANES // STRIP):
            first = top + STRIP * s
            after = first + STRIP
            rows = [work[first + SUB * g : first + SUB * (g + 1), :] for g in range(groups)]
            rows = eliminate_strip(rows, first)
            strip = jnp.concatenate(rows, axis=0)
            lane = lax.broadcasted_iota(jnp.int32, (STRIP, NB), 1)
            row = lax.broadcasted_iota(jnp.int32, (STRIP, NB), 0) + first
            strip = jnp.where((lane > row) & (lane < after), 0.0, strip)
            work[first:after, :] = jnp.where(lane < after, strip, 0.0)
            end = top + LANES
            if after < end:
                update = gram(thirds(strip), columns)[after - top :, :]
                lane = lax.broadcasted_iota(jnp.int32, (end - after, NB), 1)
                below = jnp.where((lane >= first) & (lane < after), 0.0, work[after:end, :])
                work[after:end, :] = below - update
            if between is not None:
                between(first // STRIP)
            strips.append(strip)
        if top + LANES < NB:
            upper = jnp.concatenate(strips, axis=0)
            lane = lax.broadcasted_iota(jnp.int32, (LANES, NB), 1)
            row = lax.broadcasted_iota(jnp.int32, (LANES, NB), 0) + top
            upper = jnp.where((lane > row) & (lane < top + LANES), 0.0, upper)
            update = gram(thirds(upper), slice(top + LANES, top + 2 * LANES))
            below = jnp.where(lane < top + LANES, 0.0, work[top + LANES :, :])
            work[top + LANES :, :] = below - update


def pack_kernel(own, prev, packed):
    value = own[...] - prev[...].reshape((NB, NB))
    strip_row = lax.broadcasted_iota(jnp.int32, (LANES, LANES), 0) // STRIP
    strip_col = lax.broadcasted_iota(jnp.int32, (LANES, LANES), 1) // STRIP
    packed[:LANES, :] = jnp.where(strip_row <= strip_col, value[:LANES, :LANES], value[LANES:, LANES:])
    packed[LANES : 2 * LANES, :] = value[:LANES, LANES:]
    strip = lax.broadcasted_iota(jnp.int32, (STRIP, LANES), 1) // STRIP
    diagonal = jnp.zeros((STRIP, LANES), jnp.float32)
    for i in range(LANES // STRIP):
        rows = value[LANES + STRIP * i : LANES + STRIP * (i + 1), LANES:]
        diagonal = jnp.where(strip == i, rows, diagonal)
    packed[2 * LANES :, :] = diagonal


def first_kernel(row_index, kept, one, two, three, inverse):
    packed = jnp.where(row_index[0] < ACROSS, kept[...], one[...] + two[...] + three[...])
    strip_row = lax.broadcasted_iota(jnp.int32, (LANES, LANES), 0) // STRIP
    strip_col = lax.broadcasted_iota(jnp.int32, (LANES, LANES), 1) // STRIP
    mixed = packed[:LANES, :]
    diagonal = jnp.concatenate([packed[2 * LANES :, :]] * (LANES // STRIP), axis=0)
    inverse[:LANES, :LANES] = mixed
    inverse[:LANES, LANES:] = packed[LANES : 2 * LANES, :]
    inverse[LANES:, :LANES] = jnp.zeros((LANES, LANES), jnp.float32)
    inverse[LANES:, LANES:] = jnp.where(strip_row < strip_col, mixed.T, diagonal)
    invert_factor(inverse)


def second_kernel(
    row_index, inverse0, head, own, prev, factor, trailing,
    work, before, middle, left, right, tail, arrive, leave,
):
    fetch = pltpu.make_async_copy(prev, before, arrive)
    fetch.start()
    x0 = inverse0[...]
    half = head.shape[0] // 2
    pick = lambda at, source: head[pl.ds(at, half), source].reshape((NB, NB))
    w1 = dot(x0, pick(0, 0), (1, 0))
    work[...] = pick(half, 0) - dot(w1, w1, (0, 0))
    w2 = dot(x0, pick(0, 1), (1, 1))
    cross = pick(half, 1) - dot(w2, w1, (0, 0))
    rows_here = own.shape[0]
    steps = LANES // STRIP
    piece = rows_here // steps
    row = row_index[0] * rows_here + lax.broadcasted_iota(jnp.int32, (rows_here, NB), 0)
    window = []
    writes = [
        pltpu.make_async_copy(left, factor.at[:, pl.ds(0, NB)], leave.at[0]),
        pltpu.make_async_copy(right, factor.at[:, pl.ds(NB, NB)], leave.at[1]),
        pltpu.make_async_copy(tail, trailing, leave.at[2]),
    ]

    def between(s):
        at = pl.ds(s % steps * piece, piece)
        if s == 0:
            fetch.wait()
        if s < steps:
            lower = dot(own[at, :NB] - before[at, :NB], x0, (1, 1))
            left[at, :] = lower
            middle[at, :] = own[at, NB:PANELW] - before[at, NB:PANELW] - dot(lower, w1, (1, 0))
            tail[at, :] = own[at, PANELW:] - before[at, PANELW:] - dot(lower, w2, (1, 0))
            return
        if s == steps:
            writes[0].start()
            window.append(dot(work[:LANES, :LANES], cross[:, :LANES], (1, 1)))
        lower = dot(middle[at, :LANES], work[:LANES, :LANES], (1, 1))
        right[at, :LANES] = jnp.where(row[s % steps * piece :][:piece, :LANES] >= NB, lower, 0.0)
        tail[at, :] = tail[at, :] - dot(lower, window[0], (1, 0))

    invert_factor(work, between)
    x1 = work[LANES:, :]
    rest = dot(x1, cross, (1, 1))
    lower = dot(middle[...], x1, (1, 1))
    right[:, LANES:] = jnp.where(row[:, :LANES] >= NB, lower, 0.0)
    writes[1].start()
    tail[...] = jnp.where(row >= PANELW, tail[...] - dot(lower, rest, (1, 0)), 0.0)
    writes[2].start()
    for write in writes:
        write.wait()


def exchange(blocks):
    return lax.all_to_all(blocks, "row", 0, 0, tiled=True)


def head_shares(block, row_index, count):
    side = jnp.concatenate([block[:NB, :NB], block[:NB, NB:PANELW]], axis=0)
    mine = jnp.where(row_index == 1, side, block[:, NB:PANELW])
    return mine.reshape(count, -1, NB)


def per_device(schur_own, outgoing):
    own = schur_own[0]
    out = outgoing[0]
    rows_here = own.shape[0]
    count = lax.axis_size("row")
    row_index = lax.axis_index("row").astype(jnp.int32)
    pairs = [(s, s + 1) for s in range(lax.axis_size("slab") - 1)]
    vmem = pl.BlockSpec(memory_space=pltpu.VMEM)
    smem = pl.BlockSpec(memory_space=pltpu.SMEM)
    params = pltpu.CompilerParams(vmem_limit_bytes=VMEM_BYTES)

    part = (PANELW // count, NB // count)
    corner = out[:NB, :NB].reshape(count, part[1], NB)
    sent = jnp.concatenate([head_shares(out, row_index, count), corner], axis=1)
    came = lax.ppermute(sent, "slab", pairs)
    shares = exchange(head_shares(own, row_index, count) - came[:, : part[0]])[:2]
    packed_rows = 2 * LANES + STRIP
    packed = pl.pallas_call(
        pack_kernel,
        grid=(1,),
        out_shape=jax.ShapeDtypeStruct((packed_rows, LANES), jnp.float32),
        in_specs=[
            pl.BlockSpec((NB, NB), lambda i: (0, 0)),
            pl.BlockSpec((count, part[1], NB), lambda i: (0, part[0] // part[1], 0)),
        ],
        out_specs=pl.BlockSpec((packed_rows, LANES), lambda i: (0, 0)),
        compiler_params=params,
        name="pack_corner",
    )(own, came)
    along = [lax.ppermute(packed, "row", [(0, d)]) for d in (2, 1, 3)]
    kept = jnp.where(row_index == 0, packed, along[0] + along[1] + along[2])
    down = [
        lax.ppermute(kept, "row", [(x, ACROSS * d + x) for x in range(ACROSS)]) for d in (2, 1, 3)
    ]
    head = exchange(jnp.broadcast_to(shares[None], (count,) + shares.shape))
    out, _ = lax.optimization_barrier((out, kept))
    prev = lax.ppermute(out, "slab", pairs)

    inverse0 = pl.pallas_call(
        first_kernel,
        out_shape=jax.ShapeDtypeStruct((NB, NB), jnp.float32),
        in_specs=[smem] + [vmem] * 4,
        out_specs=vmem,
        compiler_params=params,
        cost_estimate=pl.CostEstimate(
            flops=400 * NB**3, bytes_accessed=8 * NB**2, transcendentals=NB),
        name="panel_inverse",
    )(row_index[None], kept, *down)

    factor, trailing = pl.pallas_call(
        second_kernel,
        out_shape=(
            jax.ShapeDtypeStruct((rows_here, PANELW), jnp.float32),
            jax.ShapeDtypeStruct((rows_here, COLS - PANELW), jnp.float32),
        ),
        in_specs=[smem] + [vmem] * 3 + [pl.BlockSpec(memory_space=pl.ANY)],
        out_specs=(pl.BlockSpec(memory_space=pl.ANY), pl.BlockSpec(memory_space=pl.ANY)),
        scratch_shapes=[
            pltpu.VMEM((NB, NB), jnp.float32),
            pltpu.VMEM((rows_here, COLS), jnp.float32),
        ]
        + [pltpu.VMEM((rows_here, NB), jnp.float32)] * 4
        + [pltpu.SemaphoreType.DMA, pltpu.SemaphoreType.DMA((3,))],
        compiler_params=params,
        name="panel_update",
    )(row_index[None], inverse0, head, own, prev)
    return factor[None], trailing[None]


def solution(mesh):
    specs = (P("slab", "row", None), P("slab", "row", None))
    return jax.shard_map(
        per_device, mesh=mesh, in_specs=specs, out_specs=specs, check_vma=False
    )
```

```python
import jax
import jax.numpy as jnp
from jax import lax
from jax.experimental import pallas as pl
from jax.experimental.pallas import tpu as pltpu
from jax.sharding import PartitionSpec as P

NB = 256
PANELW = 512
COLS = 768
ACROSS = 4
STRIP = 32
SUB = 8
LANES = 128
VMEM_BYTES = 48 * 1024 * 1024


def dot(a, b, contract):
    return lax.dot_general(
        a, b, ((contract[:1], contract[1:]), ((), ())),
        precision=lax.Precision.HIGHEST, preferred_element_type=jnp.float32,
    )


def eliminate_strip(rows, first):
    groups = len(rows)
    lane = lax.broadcasted_iota(jnp.int32, (SUB, NB), 1)
    sub = lax.broadcasted_iota(jnp.int32, (SUB, NB), 0)
    for t in range(groups):
        col = first + SUB * t
        in_block = (lane >= col) & (lane < col + SUB)
        columns = [
            [jnp.broadcast_to(rows[g][:, col + j : col + j + 1], (SUB, LANES)) for j in range(SUB)]
            for g in range(t, groups)
        ]
        a = [
            [jnp.broadcast_to(columns[0][k][i : i + 1, :], (SUB, LANES)) if i >= k else None
             for k in range(SUB)]
            for i in range(SUB)
        ]
        start = jnp.where(in_block, (lane == col + sub).astype(jnp.float32), rows[t])
        u = [jnp.broadcast_to(start[i : i + 1, :], (SUB, NB)) for i in range(SUB)]
        inv = [None] * SUB
        low = [[None] * SUB for _ in range(SUB)]
        for j in range(0, SUB, 2):
            p, q = a[j][j], a[j + 1][j]
            det = p * a[j + 1][j + 1] - q * q
            inv[j] = lax.rsqrt(p)
            inv[j + 1] = (p * inv[j]) * lax.rsqrt(det)
            for k in range(j + 1, SUB):
                low[k][j] = a[k][j] * inv[j]
            for k in range(j + 2, SUB):
                low[k][j + 1] = (a[k][j + 1] - low[k][j] * low[j + 1][j]) * inv[j + 1]
                for m in range(j + 2, k + 1):
                    a[k][m] = a[k][m] - low[k][j] * low[m][j]
                    a[k][m] = a[k][m] - low[k][j + 1] * low[m][j + 1]
        wide = lambda x: jnp.concatenate([x, x], axis=1)
        for j in range(SUB):
            u[j] = u[j] * wide(inv[j])
            for k in range(j + 1, SUB):
                u[k] = u[k] - wide(low[k][j]) * u[j]
        packed = u[0]
        for j in range(1, SUB):
            packed = jnp.where(sub == j, u[j], packed)
        rows[t] = packed
        for g in range(t + 1, groups):
            col_g = columns[g - t]
            total = jnp.where(in_block, 0.0, rows[g])
            for j in range(SUB):
                col_g[j] = col_g[j] * inv[j]
                for k in range(j + 1, SUB):
                    col_g[k] = col_g[k] - col_g[j] * low[k][j]
                total = total - wide(col_g[j]) * u[j]
            rows[g] = total
    return rows


def thirds(x):
    high = x.astype(jnp.bfloat16)
    rest = x - high.astype(jnp.float32)
    middle = rest.astype(jnp.bfloat16)
    return high, middle, (rest - middle.astype(jnp.float32)).astype(jnp.bfloat16)


def gram(parts, columns):
    high, middle, low = parts
    left = jnp.concatenate([x[:, columns] for x in (high, high, middle, high, low, middle)], axis=0)
    right = jnp.concatenate([high, middle, high, low, high, middle], axis=0)
    return lax.dot_general(
        left, right, (((0,), (0,)), ((), ())), preferred_element_type=jnp.float32
    )


def invert_factor(work, between=None):
    groups = STRIP // SUB
    for half in range(NB // LANES):
        top = half * LANES
        columns = slice(top, top + LANES)
        strips = []
        for s in range(LANES // STRIP):
            first = top + STRIP * s
            after = first + STRIP
            rows = [work[first + SUB * g : first + SUB * (g + 1), :] for g in range(groups)]
            rows = eliminate_strip(rows, first)
            strip = jnp.concatenate(rows, axis=0)
            lane = lax.broadcasted_iota(jnp.int32, (STRIP, NB), 1)
            row = lax.broadcasted_iota(jnp.int32, (STRIP, NB), 0) + first
            strip = jnp.where((lane > row) & (lane < after), 0.0, strip)
            work[first:after, :] = jnp.where(lane < after, strip, 0.0)
            end = top + LANES
            if after < end:
                update = gram(thirds(strip), columns)[after - top :, :]
                lane = lax.broadcasted_iota(jnp.int32, (end - after, NB), 1)
                below = jnp.where((lane >= first) & (lane < after), 0.0, work[after:end, :])
                work[after:end, :] = below - update
            if between is not None:
                between(first // STRIP)
            strips.append(strip)
        if top + LANES < NB:
            upper = jnp.concatenate(strips, axis=0)
            lane = lax.broadcasted_iota(jnp.int32, (LANES, NB), 1)
            row = lax.broadcasted_iota(jnp.int32, (LANES, NB), 0) + top
            upper = jnp.where((lane > row) & (lane < top + LANES), 0.0, upper)
            update = gram(thirds(upper), slice(top + LANES, top + 2 * LANES))
            below = jnp.where(lane < top + LANES, 0.0, work[top + LANES :, :])
            work[top + LANES :, :] = below - update


def pack_kernel(own, prev, packed):
    value = own[...] - prev[...].reshape((NB, NB))
    strip_row = lax.broadcasted_iota(jnp.int32, (LANES, LANES), 0) // STRIP
    strip_col = lax.broadcasted_iota(jnp.int32, (LANES, LANES), 1) // STRIP
    packed[:LANES, :] = jnp.where(strip_row <= strip_col, value[:LANES, :LANES], value[LANES:, LANES:])
    packed[LANES : 2 * LANES, :] = value[:LANES, LANES:]
    strip = lax.broadcasted_iota(jnp.int32, (STRIP, LANES), 1) // STRIP
    diagonal = jnp.zeros((STRIP, LANES), jnp.float32)
    for i in range(LANES // STRIP):
        rows = value[LANES + STRIP * i : LANES + STRIP * (i + 1), LANES:]
        diagonal = jnp.where(strip == i, rows, diagonal)
    packed[2 * LANES :, :] = diagonal


def first_kernel(row_index, kept, one, two, three, inverse):
    packed = jnp.where(row_index[0] < ACROSS, kept[...], one[...] + two[...] + three[...])
    strip_row = lax.broadcasted_iota(jnp.int32, (LANES, LANES), 0) // STRIP
    strip_col = lax.broadcasted_iota(jnp.int32, (LANES, LANES), 1) // STRIP
    mixed = packed[:LANES, :]
    diagonal = jnp.concatenate([packed[2 * LANES :, :]] * (LANES // STRIP), axis=0)
    inverse[:LANES, :LANES] = mixed
    inverse[:LANES, LANES:] = packed[LANES : 2 * LANES, :]
    inverse[LANES:, :LANES] = jnp.zeros((LANES, LANES), jnp.float32)
    inverse[LANES:, LANES:] = jnp.where(strip_row < strip_col, mixed.T, diagonal)
    invert_factor(inverse)


def second_kernel(
    row_index, inverse0, head, own, prev, factor, trailing,
    work, before, middle, left, right, tail, arrive, leave,
):
    fetch = pltpu.make_async_copy(prev, before, arrive)
    fetch.start()
    x0 = inverse0[...]
    half = head.shape[0] // 2
    pick = lambda at, source: head[pl.ds(at, half), source].reshape((NB, NB))
    w1 = dot(x0, pick(0, 0), (1, 0))
    work[...] = pick(half, 0) - dot(w1, w1, (0, 0))
    w2 = dot(x0, pick(0, 1), (1, 1))
    cross = pick(half, 1) - dot(w2, w1, (0, 0))
    rows_here = own.shape[0]
    steps = LANES // STRIP
    piece = rows_here // steps
    row = row_index[0] * rows_here + lax.broadcasted_iota(jnp.int32, (rows_here, NB), 0)
    window = []
    writes = [
        pltpu.make_async_copy(left, factor.at[:, pl.ds(0, NB)], leave.at[0]),
        pltpu.make_async_copy(right, factor.at[:, pl.ds(NB, NB)], leave.at[1]),
        pltpu.make_async_copy(tail, trailing, leave.at[2]),
    ]

    def between(s):
        at = pl.ds(s % steps * piece, piece)
        if s == 0:
            fetch.wait()
        if s < steps:
            lower = dot(own[at, :NB] - before[at, :NB], x0, (1, 1))
            left[at, :] = lower
            middle[at, :] = own[at, NB:PANELW] - before[at, NB:PANELW] - dot(lower, w1, (1, 0))
            tail[at, :] = own[at, PANELW:] - before[at, PANELW:] - dot(lower, w2, (1, 0))
            return
        if s == steps:
            writes[0].start()
            window.append(dot(work[:LANES, :LANES], cross[:, :LANES], (1, 1)))
        lower = dot(middle[at, :LANES], work[:LANES, :LANES], (1, 1))
        right[at, :LANES] = jnp.where(row[s % steps * piece :][:piece, :LANES] >= NB, lower, 0.0)
        tail[at, :] = tail[at, :] - dot(lower, window[0], (1, 0))

    invert_factor(work, between)
    x1 = work[LANES:, :]
    rest = dot(x1, cross, (1, 1))
    lower = dot(middle[...], x1, (1, 1))
    right[:, LANES:] = jnp.where(row[:, :LANES] >= NB, lower, 0.0)
    writes[1].start()
    tail[...] = jnp.where(row >= PANELW, tail[...] - dot(lower, rest, (1, 0)), 0.0)
    writes[2].start()
    for write in writes:
        write.wait()


def exchange(blocks):
    return lax.all_to_all(blocks, "row", 0, 0, tiled=True)


def head_shares(block, row_index, count):
    side = jnp.concatenate([block[:NB, :NB], block[:NB, NB:PANELW]], axis=0)
    mine = jnp.where(row_index == 1, side, block[:, NB:PANELW])
    return mine.reshape(count, -1, NB)


def per_device(schur_own, outgoing):
    own = schur_own[0]
    out = outgoing[0]
    rows_here = own.shape[0]
    count = lax.axis_size("row")
    row_index = lax.axis_index("row").astype(jnp.int32)
    pairs = [(s, s + 1) for s in range(lax.axis_size("slab") - 1)]
    vmem = pl.BlockSpec(memory_space=pltpu.VMEM)
    smem = pl.BlockSpec(memory_space=pltpu.SMEM)
    params = pltpu.CompilerParams(vmem_limit_bytes=VMEM_BYTES)

    part = (PANELW // count, NB // count)
    corner = out[:NB, :NB].reshape(count, part[1], NB)
    sent = jnp.concatenate([head_shares(out, row_index, count), corner], axis=1)
    came = lax.ppermute(sent, "slab", pairs)
    mine = head_shares(own, row_index, count) - came[:, : part[0]]
    mine, came = lax.optimization_barrier((mine, came))
    shares = exchange(mine)[:2]
    packed_rows = 2 * LANES + STRIP
    packed = pl.pallas_call(
        pack_kernel,
        grid=(1,),
        out_shape=jax.ShapeDtypeStruct((packed_rows, LANES), jnp.float32),
        in_specs=[
            pl.BlockSpec((NB, NB), lambda i: (0, 0)),
            pl.BlockSpec((count, part[1], NB), lambda i: (0, part[0] // part[1], 0)),
        ],
        out_specs=pl.BlockSpec((packed_rows, LANES), lambda i: (0, 0)),
        compiler_params=params,
        name="pack_corner",
    )(own, came)
    along = [lax.ppermute(packed, "row", [(0, d)]) for d in (2, 1, 3)]
    kept = jnp.where(row_index == 0, packed, along[0] + along[1] + along[2])
    out, _ = lax.optimization_barrier((out, kept))
    prev = lax.ppermute(out, "slab", pairs)
    down = [
        lax.ppermute(kept, "row", [(x, ACROSS * d + x) for x in range(ACROSS)]) for d in (2, 1, 3)
    ]
    *down, shares = lax.optimization_barrier((*down, shares))
    head = exchange(jnp.broadcast_to(shares[None], (count,) + shares.shape))

    inverse0 = pl.pallas_call(
        first_kernel,
        out_shape=jax.ShapeDtypeStruct((NB, NB), jnp.float32),
        in_specs=[smem] + [vmem] * 4,
        out_specs=vmem,
        compiler_params=params,
        cost_estimate=pl.CostEstimate(
            flops=400 * NB**3, bytes_accessed=8 * NB**2, transcendentals=NB),
        name="panel_inverse",
    )(row_index[None], kept, *down)

    factor, trailing = pl.pallas_call(
        second_kernel,
        out_shape=(
            jax.ShapeDtypeStruct((rows_here, PANELW), jnp.float32),
            jax.ShapeDtypeStruct((rows_here, COLS - PANELW), jnp.float32),
        ),
        in_specs=[smem] + [vmem] * 3 + [pl.BlockSpec(memory_space=pl.ANY)],
        out_specs=(pl.BlockSpec(memory_space=pl.ANY), pl.BlockSpec(memory_space=pl.ANY)),
        scratch_shapes=[
            pltpu.VMEM((NB, NB), jnp.float32),
            pltpu.VMEM((rows_here, COLS), jnp.float32),
        ]
        + [pltpu.VMEM((rows_here, NB), jnp.float32)] * 4
        + [pltpu.SemaphoreType.DMA, pltpu.SemaphoreType.DMA((3,))],
        compiler_params=params,
        name="panel_update",
    )(row_index[None], inverse0, head, own, prev)
    return factor[None], trailing[None]


def solution(mesh):
    specs = (P("slab", "row", None), P("slab", "row", None))
    return jax.shard_map(
        per_device, mesh=mesh, in_specs=specs, out_specs=specs, check_vma=False
    )
```

```python
import jax
import jax.numpy as jnp
from jax import lax
from jax.experimental import pallas as pl
from jax.experimental.pallas import tpu as pltpu
from jax.sharding import PartitionSpec as P

NB = 256
PANELW = 512
COLS = 768
PART = 16
STRIP = 32
SUB = 8
LANES = 128
VMEM_BYTES = 48 * 1024 * 1024


def dot(a, b, contract):
    return lax.dot_general(
        a, b, ((contract[:1], contract[1:]), ((), ())),
        precision=lax.Precision.HIGHEST, preferred_element_type=jnp.float32,
    )


def eliminate_strip(rows, first):
    groups = len(rows)
    lane = lax.broadcasted_iota(jnp.int32, (SUB, NB), 1)
    sub = lax.broadcasted_iota(jnp.int32, (SUB, NB), 0)
    for t in range(groups):
        col = first + SUB * t
        in_block = (lane >= col) & (lane < col + SUB)
        columns = [
            [jnp.broadcast_to(rows[g][:, col + j : col + j + 1], (SUB, LANES)) for j in range(SUB)]
            for g in range(t, groups)
        ]
        a = [
            [jnp.broadcast_to(columns[0][k][i : i + 1, :], (SUB, LANES)) if i >= k else None
             for k in range(SUB)]
            for i in range(SUB)
        ]
        start = jnp.where(in_block, (lane == col + sub).astype(jnp.float32), rows[t])
        u = [jnp.broadcast_to(start[i : i + 1, :], (SUB, NB)) for i in range(SUB)]
        inv = [None] * SUB
        low = [[None] * SUB for _ in range(SUB)]
        for j in range(0, SUB, 2):
            p, q = a[j][j], a[j + 1][j]
            det = p * a[j + 1][j + 1] - q * q
            inv[j] = lax.rsqrt(p)
            inv[j + 1] = (p * inv[j]) * lax.rsqrt(det)
            for k in range(j + 1, SUB):
                low[k][j] = a[k][j] * inv[j]
            for k in range(j + 2, SUB):
                low[k][j + 1] = (a[k][j + 1] - low[k][j] * low[j + 1][j]) * inv[j + 1]
                for m in range(j + 2, k + 1):
                    a[k][m] = a[k][m] - low[k][j] * low[m][j]
                    a[k][m] = a[k][m] - low[k][j + 1] * low[m][j + 1]
        wide = lambda x: jnp.concatenate([x, x], axis=1)
        for j in range(SUB):
            u[j] = u[j] * wide(inv[j])
            for k in range(j + 1, SUB):
                u[k] = u[k] - wide(low[k][j]) * u[j]
        packed = u[0]
        for j in range(1, SUB):
            packed = jnp.where(sub == j, u[j], packed)
        rows[t] = packed
        for g in range(t + 1, groups):
            col_g = columns[g - t]
            total = jnp.where(in_block, 0.0, rows[g])
            for j in range(SUB):
                col_g[j] = col_g[j] * inv[j]
                for k in range(j + 1, SUB):
                    col_g[k] = col_g[k] - col_g[j] * low[k][j]
                total = total - wide(col_g[j]) * u[j]
            rows[g] = total
    return rows


def thirds(x):
    high = x.astype(jnp.bfloat16)
    rest = x - high.astype(jnp.float32)
    middle = rest.astype(jnp.bfloat16)
    return high, middle, (rest - middle.astype(jnp.float32)).astype(jnp.bfloat16)


def gram(parts, columns):
    high, middle, low = parts
    left = jnp.concatenate([x[:, columns] for x in (high, high, middle, high, low, middle)], axis=0)
    right = jnp.concatenate([high, middle, high, low, high, middle], axis=0)
    return lax.dot_general(
        left, right, (((0,), (0,)), ((), ())), preferred_element_type=jnp.float32
    )


def invert_factor(work, between=None):
    groups = STRIP // SUB
    for half in range(NB // LANES):
        top = half * LANES
        columns = slice(top, top + LANES)
        strips = []
        for s in range(LANES // STRIP):
            first = top + STRIP * s
            after = first + STRIP
            rows = [work[first + SUB * g : first + SUB * (g + 1), :] for g in range(groups)]
            rows = eliminate_strip(rows, first)
            strip = jnp.concatenate(rows, axis=0)
            lane = lax.broadcasted_iota(jnp.int32, (STRIP, NB), 1)
            row = lax.broadcasted_iota(jnp.int32, (STRIP, NB), 0) + first
            strip = jnp.where((lane > row) & (lane < after), 0.0, strip)
            work[first:after, :] = jnp.where(lane < after, strip, 0.0)
            end = top + LANES
            if after < end:
                update = gram(thirds(strip), columns)[after - top :, :]
                lane = lax.broadcasted_iota(jnp.int32, (end - after, NB), 1)
                below = jnp.where((lane >= first) & (lane < after), 0.0, work[after:end, :])
                work[after:end, :] = below - update
            if between is not None:
                between(first // STRIP)
            strips.append(strip)
        if top + LANES < NB:
            upper = jnp.concatenate(strips, axis=0)
            lane = lax.broadcasted_iota(jnp.int32, (LANES, NB), 1)
            row = lax.broadcasted_iota(jnp.int32, (LANES, NB), 0) + top
            upper = jnp.where((lane > row) & (lane < top + LANES), 0.0, upper)
            update = gram(thirds(upper), slice(top + LANES, top + 2 * LANES))
            below = jnp.where(lane < top + LANES, 0.0, work[top + LANES :, :])
            work[top + LANES :, :] = below - update


def block_of(shares):
    return shares.reshape((NB, NB))


def first_kernel(mixed, inverse):
    inverse[...] = block_of(mixed[:, :PART])
    invert_factor(inverse)


def second_kernel(
    row_index, inverse0, mixed, rest, own, prev, factor, trailing,
    work, before, middle, left, right, tail, arrive, leave,
):
    fetch = pltpu.make_async_copy(prev, before, arrive)
    fetch.start()
    x0 = inverse0[...]
    strip_row = lax.broadcasted_iota(jnp.int32, (NB, NB), 0) // STRIP
    strip_col = lax.broadcasted_iota(jnp.int32, (NB, NB), 1) // STRIP
    diagonal = mixed[: STRIP // SUB, PART:].reshape((STRIP, NB))
    diagonal = jnp.concatenate([diagonal] * (NB // STRIP), axis=0)
    block = jnp.where(strip_row < strip_col, block_of(mixed[:, :PART]).T, diagonal)
    w1 = dot(x0, block_of(rest[:, 0]), (1, 0))
    work[...] = block - dot(w1, w1, (0, 0))
    w2 = dot(x0, block_of(rest[:, 1]), (1, 1))
    cross = block_of(rest[:, 2]) - dot(w2, w1, (0, 0))
    rows_here = own.shape[0]
    steps = LANES // STRIP
    piece = rows_here // steps
    row = row_index[0] * rows_here + lax.broadcasted_iota(jnp.int32, (rows_here, NB), 0)
    window = []
    writes = [
        pltpu.make_async_copy(left, factor.at[:, pl.ds(0, NB)], leave.at[0]),
        pltpu.make_async_copy(right, factor.at[:, pl.ds(NB, NB)], leave.at[1]),
        pltpu.make_async_copy(tail, trailing, leave.at[2]),
    ]

    def between(s):
        at = pl.ds(s % steps * piece, piece)
        if s == 0:
            fetch.wait()
        if s < steps:
            lower = dot(own[at, :NB] - before[at, :NB], x0, (1, 1))
            left[at, :] = lower
            middle[at, :] = own[at, NB:PANELW] - before[at, NB:PANELW] - dot(lower, w1, (1, 0))
            tail[at, :] = own[at, PANELW:] - before[at, PANELW:] - dot(lower, w2, (1, 0))
            return
        if s == steps:
            writes[0].start()
            window.append(dot(work[:LANES, :LANES], cross[:, :LANES], (1, 1)))
        lower = dot(middle[at, :LANES], work[:LANES, :LANES], (1, 1))
        right[at, :LANES] = jnp.where(row[s % steps * piece :][:piece, :LANES] >= NB, lower, 0.0)
        tail[at, :] = tail[at, :] - dot(lower, window[0], (1, 0))

    invert_factor(work, between)
    x1 = work[LANES:, :]
    window.append(dot(x1, cross, (1, 1)))
    lower = dot(middle[...], x1, (1, 1))
    right[:, LANES:] = jnp.where(row[:, :LANES] >= NB, lower, 0.0)
    writes[1].start()
    tail[...] = jnp.where(row >= PANELW, tail[...] - dot(lower, window[1], (1, 0)), 0.0)
    writes[2].start()
    for write in writes:
        write.wait()


def exchange(blocks):
    return lax.all_to_all(blocks, "row", 0, 0, tiled=True)


def head_shares(block, row_index, count):
    first, second = block[:NB, :NB], block[NB:PANELW, NB:PANELW]
    strip_row = jnp.arange(NB)[:, None] // STRIP
    strip_col = jnp.arange(NB)[None, :] // STRIP
    mixed = jnp.where((strip_row <= strip_col) | (row_index == 1), first, second)
    strips = second.reshape(NB // STRIP, STRIP, NB)
    own_strip = jnp.arange(NB // STRIP)[:, None, None] == strip_col[None]
    diagonal = jnp.sum(jnp.where(own_strip, strips, 0.0), axis=0).reshape(-1, SUB, NB)
    diagonal = jnp.pad(diagonal, ((0, count - diagonal.shape[0]), (0, 0), (0, 0)))
    parts = [mixed.reshape(count, PART, NB), diagonal, block[:NB, NB:PANELW].reshape(count, PART, NB)]
    return jnp.concatenate(parts, axis=1)


def copies(share, count):
    return jnp.broadcast_to(share[None], (count,) + share.shape)


def per_device(schur_own, outgoing):
    own = schur_own[0]
    out = outgoing[0]
    rows_here = own.shape[0]
    count = lax.axis_size("row")
    row_index = lax.axis_index("row").astype(jnp.int32)
    pairs = [(s, s + 1) for s in range(lax.axis_size("slab") - 1)]
    vmem = pl.BlockSpec(memory_space=pltpu.VMEM)
    smem = pl.BlockSpec(memory_space=pltpu.SMEM)
    params = pltpu.CompilerParams(vmem_limit_bytes=VMEM_BYTES)

    sent = head_shares(out, row_index, count)
    came = lax.ppermute(sent, "slab", pairs)
    own, _ = lax.optimization_barrier((own, sent))
    kept = head_shares(own, row_index, count)
    out, _ = lax.optimization_barrier((out, kept))
    prev = lax.ppermute(out, "slab", pairs)
    shares = exchange(kept - came)[:2]
    mixed = exchange(copies(shares[0, : PART + SUB], count))
    rest = jnp.stack([shares[0, PART + SUB :], shares[1, :PART], shares[1, PART + SUB :]])
    rest, mixed = lax.optimization_barrier((copies(rest, count), mixed))
    rest = exchange(rest)

    inverse0 = pl.pallas_call(
        first_kernel,
        out_shape=jax.ShapeDtypeStruct((NB, NB), jnp.float32),
        in_specs=[vmem],
        out_specs=vmem,
        compiler_params=params,
        cost_estimate=pl.CostEstimate(
            flops=400 * NB**3, bytes_accessed=8 * NB**2, transcendentals=NB),
        name="panel_inverse",
    )(mixed)

    factor, trailing = pl.pallas_call(
        second_kernel,
        out_shape=(
            jax.ShapeDtypeStruct((rows_here, PANELW), jnp.float32),
            jax.ShapeDtypeStruct((rows_here, COLS - PANELW), jnp.float32),
        ),
        in_specs=[smem] + [vmem] * 4 + [pl.BlockSpec(memory_space=pl.ANY)],
        out_specs=(pl.BlockSpec(memory_space=pl.ANY), pl.BlockSpec(memory_space=pl.ANY)),
        scratch_shapes=[
            pltpu.VMEM((NB, NB), jnp.float32),
            pltpu.VMEM((rows_here, COLS), jnp.float32),
        ]
        + [pltpu.VMEM((rows_here, NB), jnp.float32)] * 4
        + [pltpu.SemaphoreType.DMA, pltpu.SemaphoreType.DMA((3,))],
        compiler_params=params,
        name="panel_update",
    )(row_index[None], inverse0, mixed, rest, own, prev)
    return factor[None], trailing[None]


def solution(mesh):
    specs = (P("slab", "row", None), P("slab", "row", None))
    return jax.shard_map(
        per_device, mesh=mesh, in_specs=specs, out_specs=specs, check_vma=False
    )
```

```python
import jax
import jax.numpy as jnp
from jax import lax
from jax.experimental import pallas as pl
from jax.experimental.pallas import tpu as pltpu
from jax.sharding import PartitionSpec as P

NB = 256
PANELW = 512
COLS = 768
PART = 16
STRIP = 32
SUB = 8
LANES = 128
VMEM_BYTES = 48 * 1024 * 1024


def dot(a, b, contract):
    return lax.dot_general(
        a, b, ((contract[:1], contract[1:]), ((), ())),
        precision=lax.Precision.HIGHEST, preferred_element_type=jnp.float32,
    )


def eliminate_strip(rows, first):
    groups = len(rows)
    lane = lax.broadcasted_iota(jnp.int32, (SUB, NB), 1)
    sub = lax.broadcasted_iota(jnp.int32, (SUB, NB), 0)
    for t in range(groups):
        col = first + SUB * t
        in_block = (lane >= col) & (lane < col + SUB)
        columns = [
            [jnp.broadcast_to(rows[g][:, col + j : col + j + 1], (SUB, LANES)) for j in range(SUB)]
            for g in range(t, groups)
        ]
        a = [
            [jnp.broadcast_to(columns[0][k][i : i + 1, :], (SUB, LANES)) if i >= k else None
             for k in range(SUB)]
            for i in range(SUB)
        ]
        start = jnp.where(in_block, (lane == col + sub).astype(jnp.float32), rows[t])
        u = [jnp.broadcast_to(start[i : i + 1, :], (SUB, NB)) for i in range(SUB)]
        inv = [None] * SUB
        low = [[None] * SUB for _ in range(SUB)]
        for j in range(0, SUB, 4):
            p, q, r = a[j][j], a[j + 1][j], a[j + 1][j + 1]
            det = p * r - q * q
            left = {m: r * a[m][j] - q * a[m][j + 1] for m in (j + 2, j + 3)}
            right = {m: p * a[m][j + 1] - q * a[m][j] for m in (j + 2, j + 3)}
            scaled = lambda m, n: det * a[m][n] - (a[n][j] * left[m] + a[n][j + 1] * right[m])
            third = scaled(j + 2, j + 2)
            cross = scaled(j + 3, j + 2)
            both = third * scaled(j + 3, j + 3) - cross * cross
            inv[j] = lax.rsqrt(p)
            root, root_third = lax.rsqrt(det), lax.rsqrt(third)
            inv[j + 1] = (p * inv[j]) * root
            inv[j + 2] = (det * root) * root_third
            inv[j + 3] = ((det * root) * (third * root_third)) * lax.rsqrt(both)
            for c in range(j, j + 4):
                for k in range(c + 1, SUB):
                    value = a[k][c]
                    for e in range(j, c):
                        value = value - low[k][e] * low[c][e]
                    low[k][c] = value * inv[c]
            for k in range(j + 4, SUB):
                for m in range(j + 4, k + 1):
                    for c in range(j, j + 4):
                        a[k][m] = a[k][m] - low[k][c] * low[m][c]
        wide = lambda x: jnp.concatenate([x, x], axis=1)
        for j in range(SUB):
            u[j] = u[j] * wide(inv[j])
            for k in range(j + 1, SUB):
                u[k] = u[k] - wide(low[k][j]) * u[j]
        packed = u[0]
        for j in range(1, SUB):
            packed = jnp.where(sub == j, u[j], packed)
        rows[t] = packed
        for g in range(t + 1, groups):
            col_g = columns[g - t]
            total = jnp.where(in_block, 0.0, rows[g])
            for j in range(SUB):
                col_g[j] = col_g[j] * inv[j]
                for k in range(j + 1, SUB):
                    col_g[k] = col_g[k] - col_g[j] * low[k][j]
                total = total - wide(col_g[j]) * u[j]
            rows[g] = total
    return rows


def thirds(x):
    high = x.astype(jnp.bfloat16)
    rest = x - high.astype(jnp.float32)
    middle = rest.astype(jnp.bfloat16)
    return high, middle, (rest - middle.astype(jnp.float32)).astype(jnp.bfloat16)


def gram(parts, columns):
    high, middle, low = parts
    left = jnp.concatenate([x[:, columns] for x in (high, high, middle, high, low, middle)], axis=0)
    right = jnp.concatenate([high, middle, high, low, high, middle], axis=0)
    return lax.dot_general(
        left, right, (((0,), (0,)), ((), ())), preferred_element_type=jnp.float32
    )


def scales(diagonal):
    row = lax.rsqrt(diagonal)
    on_diagonal = lax.broadcasted_iota(jnp.int32, (NB, NB), 0) == lax.broadcasted_iota(
        jnp.int32, (NB, NB), 1)
    return row, jnp.sum(jnp.where(on_diagonal, row, 0.0), axis=1, keepdims=True)


def diagonal_of(block):
    on_diagonal = lax.broadcasted_iota(jnp.int32, (NB, NB), 0) == lax.broadcasted_iota(
        jnp.int32, (NB, NB), 1)
    return jnp.sum(jnp.where(on_diagonal, block, 0.0), axis=0, keepdims=True)


def invert_factor(work, scale, between=None):
    groups = STRIP // SUB
    for half in range(NB // LANES):
        top = half * LANES
        columns = slice(top, top + LANES)
        strips = []
        for s in range(LANES // STRIP):
            first = top + STRIP * s
            after = first + STRIP
            rows = [work[first + SUB * g : first + SUB * (g + 1), :] for g in range(groups)]
            rows = eliminate_strip(rows, first)
            strip = jnp.concatenate(rows, axis=0)
            lane = lax.broadcasted_iota(jnp.int32, (STRIP, NB), 1)
            row = lax.broadcasted_iota(jnp.int32, (STRIP, NB), 0) + first
            strip = jnp.where((lane > row) & (lane < after), 0.0, strip)
            work[first:after, :] = jnp.where(lane < after, strip, 0.0) * scale
            end = top + LANES
            if after < end:
                update = gram(thirds(strip), columns)[after - top :, :]
                lane = lax.broadcasted_iota(jnp.int32, (end - after, NB), 1)
                below = jnp.where((lane >= first) & (lane < after), 0.0, work[after:end, :])
                work[after:end, :] = below - update
            if between is not None:
                between(first // STRIP)
            strips.append(strip)
        if top + LANES < NB:
            upper = jnp.concatenate(strips, axis=0)
            lane = lax.broadcasted_iota(jnp.int32, (LANES, NB), 1)
            row = lax.broadcasted_iota(jnp.int32, (LANES, NB), 0) + top
            upper = jnp.where((lane > row) & (lane < top + LANES), 0.0, upper)
            update = gram(thirds(upper), slice(top + LANES, top + 2 * LANES))
            below = jnp.where(lane < top + LANES, 0.0, work[top + LANES :, :])
            work[top + LANES :, :] = below - update


def block_of(shares):
    return shares.reshape((NB, NB))


def first_kernel(mixed, inverse):
    block = block_of(mixed[:, :PART])
    row, column = scales(diagonal_of(block))
    inverse[...] = block * row * column
    invert_factor(inverse, row)


def second_kernel(
    row_index, inverse0, mixed, rest, own, prev, factor, trailing,
    work, before, middle, left, right, tail, arrive, leave,
):
    fetch = pltpu.make_async_copy(prev, before, arrive)
    fetch.start()
    x0 = inverse0[...]
    strip_row = lax.broadcasted_iota(jnp.int32, (NB, NB), 0) // STRIP
    strip_col = lax.broadcasted_iota(jnp.int32, (NB, NB), 1) // STRIP
    diagonal = mixed[: STRIP // SUB, PART:].reshape((STRIP, NB))
    diagonal = jnp.concatenate([diagonal] * (NB // STRIP), axis=0)
    block = jnp.where(strip_row < strip_col, block_of(mixed[:, :PART]).T, diagonal)
    w1 = dot(x0, block_of(rest[:, 0]), (1, 0))
    scale, column = scales(diagonal_of(diagonal) - jnp.sum(w1 * w1, axis=0, keepdims=True))
    reduced = block[:LANES] - dot(w1[:, :LANES], w1, (0, 0))
    work[:LANES, :] = reduced * scale * column[:LANES]
    w2 = dot(x0, block_of(rest[:, 1]), (1, 1))
    cross = block_of(rest[:, 2]) - dot(w2, w1, (0, 0))
    rows_here = own.shape[0]
    steps = LANES // STRIP
    piece = rows_here // steps
    row = row_index[0] * rows_here + lax.broadcasted_iota(jnp.int32, (rows_here, NB), 0)
    window = []
    writes = [
        pltpu.make_async_copy(left, factor.at[:, pl.ds(0, NB)], leave.at[0]),
        pltpu.make_async_copy(right, factor.at[:, pl.ds(NB, NB)], leave.at[1]),
        pltpu.make_async_copy(tail, trailing, leave.at[2]),
    ]

    def between(s):
        at = pl.ds(s % steps * piece, piece)
        if s == 0:
            reduced = block[LANES:] - dot(w1[:, LANES:], w1, (0, 0))
            work[LANES:, :] = reduced * scale * column[LANES:]
            fetch.wait()
        if s < steps:
            lower = dot(own[at, :NB] - before[at, :NB], x0, (1, 1))
            left[at, :] = lower
            middle[at, :] = own[at, NB:PANELW] - before[at, NB:PANELW] - dot(lower, w1, (1, 0))
            tail[at, :] = own[at, PANELW:] - before[at, PANELW:] - dot(lower, w2, (1, 0))
            return
        if s == steps:
            writes[0].start()
            window.append(dot(work[:LANES, :LANES], cross[:, :LANES], (1, 1)))
        lower = dot(middle[at, :LANES], work[:LANES, :LANES], (1, 1))
        right[at, :LANES] = jnp.where(row[s % steps * piece :][:piece, :LANES] >= NB, lower, 0.0)
        tail[at, :] = tail[at, :] - dot(lower, window[0], (1, 0))

    invert_factor(work, scale, between)
    x1 = work[LANES:, :]
    window.append(dot(x1, cross, (1, 1)))
    lower = dot(middle[...], x1, (1, 1))
    right[:, LANES:] = jnp.where(row[:, :LANES] >= NB, lower, 0.0)
    writes[1].start()
    tail[...] = jnp.where(row >= PANELW, tail[...] - dot(lower, window[1], (1, 0)), 0.0)
    writes[2].start()
    for write in writes:
        write.wait()


def exchange(blocks):
    return lax.all_to_all(blocks, "row", 0, 0, tiled=True)


def head_shares(block, row_index, count):
    first, second = block[:NB, :NB], block[NB:PANELW, NB:PANELW]
    strip_row = jnp.arange(NB)[:, None] // STRIP
    strip_col = jnp.arange(NB)[None, :] // STRIP
    mixed = jnp.where((strip_row <= strip_col) | (row_index == 1), first, second)
    strips = second.reshape(NB // STRIP, STRIP, NB)
    own_strip = jnp.arange(NB // STRIP)[:, None, None] == strip_col[None]
    diagonal = jnp.sum(jnp.where(own_strip, strips, 0.0), axis=0).reshape(-1, SUB, NB)
    diagonal = jnp.pad(diagonal, ((0, count - diagonal.shape[0]), (0, 0), (0, 0)))
    parts = [mixed.reshape(count, PART, NB), diagonal, block[:NB, NB:PANELW].reshape(count, PART, NB)]
    return jnp.concatenate(parts, axis=1)


def copies(share, count):
    return jnp.broadcast_to(share[None], (count,) + share.shape)


def per_device(schur_own, outgoing):
    own = schur_own[0]
    out = outgoing[0]
    rows_here = own.shape[0]
    count = lax.axis_size("row")
    row_index = lax.axis_index("row").astype(jnp.int32)
    pairs = [(s, s + 1) for s in range(lax.axis_size("slab") - 1)]
    vmem = pl.BlockSpec(memory_space=pltpu.VMEM)
    smem = pl.BlockSpec(memory_space=pltpu.SMEM)
    params = pltpu.CompilerParams(vmem_limit_bytes=VMEM_BYTES)

    sent = head_shares(out, row_index, count)
    came = lax.ppermute(sent, "slab", pairs)
    own, _ = lax.optimization_barrier((own, sent))
    kept = head_shares(own, row_index, count)
    out, _ = lax.optimization_barrier((out, kept))
    prev = lax.ppermute(out, "slab", pairs)
    shares = exchange(kept - came)[:2]
    mixed = exchange(copies(shares[0, : PART + SUB], count))
    rest = jnp.stack([shares[0, PART + SUB :], shares[1, :PART], shares[1, PART + SUB :]])
    rest, mixed = lax.optimization_barrier((copies(rest, count), mixed))
    rest = exchange(rest)

    inverse0 = pl.pallas_call(
        first_kernel,
        out_shape=jax.ShapeDtypeStruct((NB, NB), jnp.float32),
        in_specs=[vmem],
        out_specs=vmem,
        compiler_params=params,
        cost_estimate=pl.CostEstimate(
            flops=400 * NB**3, bytes_accessed=8 * NB**2, transcendentals=NB),
        name="panel_inverse",
    )(mixed)

    factor, trailing = pl.pallas_call(
        second_kernel,
        out_shape=(
            jax.ShapeDtypeStruct((rows_here, PANELW), jnp.float32),
            jax.ShapeDtypeStruct((rows_here, COLS - PANELW), jnp.float32),
        ),
        in_specs=[smem] + [vmem] * 4 + [pl.BlockSpec(memory_space=pl.ANY)],
        out_specs=(pl.BlockSpec(memory_space=pl.ANY), pl.BlockSpec(memory_space=pl.ANY)),
        scratch_shapes=[
            pltpu.VMEM((NB, NB), jnp.float32),
            pltpu.VMEM((rows_here, COLS), jnp.float32),
        ]
        + [pltpu.VMEM((rows_here, NB), jnp.float32)] * 4
        + [pltpu.SemaphoreType.DMA, pltpu.SemaphoreType.DMA((3,))],
        compiler_params=params,
        name="panel_update",
    )(row_index[None], inverse0, mixed, rest, own, prev)
    return factor[None], trailing[None]


def solution(mesh):
    specs = (P("slab", "row", None), P("slab", "row", None))
    return jax.shard_map(
        per_device, mesh=mesh, in_specs=specs, out_specs=specs, check_vma=False
    )
```

```python
import jax
import jax.numpy as jnp
from jax import lax
from jax.experimental import pallas as pl
from jax.experimental.pallas import tpu as pltpu
from jax.sharding import PartitionSpec as P

NB = 256
PANELW = 512
COLS = 768
PART = 16
STRIP = 32
SUB = 8
LANES = 128
VMEM_BYTES = 48 * 1024 * 1024


def dot(a, b, contract):
    return lax.dot_general(
        a, b, ((contract[:1], contract[1:]), ((), ())),
        precision=lax.Precision.HIGHEST, preferred_element_type=jnp.float32,
    )


def eliminate_strip(rows, first):
    groups = len(rows)
    lane = lax.broadcasted_iota(jnp.int32, (SUB, NB), 1)
    sub = lax.broadcasted_iota(jnp.int32, (SUB, NB), 0)
    for t in range(groups):
        col = first + SUB * t
        in_block = (lane >= col) & (lane < col + SUB)
        columns = [
            [jnp.broadcast_to(rows[g][:, col + j : col + j + 1], (SUB, LANES)) for j in range(SUB)]
            for g in range(t, groups)
        ]
        a = [
            [jnp.broadcast_to(columns[0][k][i : i + 1, :], (SUB, LANES)) if i >= k else None
             for k in range(SUB)]
            for i in range(SUB)
        ]
        start = jnp.where(in_block, (lane == col + sub).astype(jnp.float32), rows[t])
        u = [jnp.broadcast_to(start[i : i + 1, :], (SUB, NB)) for i in range(SUB)]
        inv = [None] * SUB
        low = [[None] * SUB for _ in range(SUB)]
        for j in range(0, SUB, 4):
            p, q, r = a[j][j], a[j + 1][j], a[j + 1][j + 1]
            det = p * r - q * q
            left = {m: r * a[m][j] - q * a[m][j + 1] for m in (j + 2, j + 3)}
            right = {m: p * a[m][j + 1] - q * a[m][j] for m in (j + 2, j + 3)}
            scaled = lambda m, n: det * a[m][n] - (a[n][j] * left[m] + a[n][j + 1] * right[m])
            third = scaled(j + 2, j + 2)
            cross = scaled(j + 3, j + 2)
            both = third * scaled(j + 3, j + 3) - cross * cross
            inv[j] = lax.rsqrt(p)
            root, root_third = lax.rsqrt(det), lax.rsqrt(third)
            inv[j + 1] = (p * inv[j]) * root
            inv[j + 2] = (det * root) * root_third
            inv[j + 3] = ((det * root) * (third * root_third)) * lax.rsqrt(both)
            for c in range(j, j + 4):
                for k in range(c + 1, SUB):
                    value = a[k][c]
                    for e in range(j, c):
                        value = value - low[k][e] * low[c][e]
                    low[k][c] = value * inv[c]
            for k in range(j + 4, SUB):
                for m in range(j + 4, k + 1):
                    for c in range(j, j + 4):
                        a[k][m] = a[k][m] - low[k][c] * low[m][c]
        wide = lambda x: jnp.concatenate([x, x], axis=1)
        for j in range(SUB):
            u[j] = u[j] * wide(inv[j])
            for k in range(j + 1, SUB):
                u[k] = u[k] - wide(low[k][j]) * u[j]
        packed = u[0]
        for j in range(1, SUB):
            packed = jnp.where(sub == j, u[j], packed)
        rows[t] = packed
        for g in range(t + 1, groups):
            col_g = columns[g - t]
            total = jnp.where(in_block, 0.0, rows[g])
            for j in range(SUB):
                col_g[j] = col_g[j] * inv[j]
                for k in range(j + 1, SUB):
                    col_g[k] = col_g[k] - col_g[j] * low[k][j]
                total = total - wide(col_g[j]) * u[j]
            rows[g] = total
    return rows


def thirds(x):
    high = x.astype(jnp.bfloat16)
    rest = x - high.astype(jnp.float32)
    middle = rest.astype(jnp.bfloat16)
    return high, middle, (rest - middle.astype(jnp.float32)).astype(jnp.bfloat16)


def gram(parts, columns):
    high, middle, low = parts
    left = jnp.concatenate([x[:, columns] for x in (high, high, middle, high, low, middle)], axis=0)
    right = jnp.concatenate([high, middle, high, low, high, middle], axis=0)
    return lax.dot_general(
        left, right, (((0,), (0,)), ((), ())), preferred_element_type=jnp.float32
    )


def scales(diagonal):
    row = lax.rsqrt(diagonal)
    on_diagonal = lax.broadcasted_iota(jnp.int32, (NB, NB), 0) == lax.broadcasted_iota(
        jnp.int32, (NB, NB), 1)
    return row, jnp.sum(jnp.where(on_diagonal, row, 0.0), axis=1, keepdims=True)


def diagonal_of(block):
    on_diagonal = lax.broadcasted_iota(jnp.int32, (NB, NB), 0) == lax.broadcasted_iota(
        jnp.int32, (NB, NB), 1)
    return jnp.sum(jnp.where(on_diagonal, block, 0.0), axis=0, keepdims=True)


def invert_factor(work, scale, between=None):
    groups = STRIP // SUB
    for half in range(NB // LANES):
        top = half * LANES
        columns = slice(top, top + LANES)
        strips = []
        for s in range(LANES // STRIP):
            first = top + STRIP * s
            after = first + STRIP
            rows = [work[first + SUB * g : first + SUB * (g + 1), :] for g in range(groups)]
            rows = eliminate_strip(rows, first)
            strip = jnp.concatenate(rows, axis=0)
            lane = lax.broadcasted_iota(jnp.int32, (STRIP, NB), 1)
            row = lax.broadcasted_iota(jnp.int32, (STRIP, NB), 0) + first
            strip = jnp.where((lane > row) & (lane < after), 0.0, strip)
            work[first:after, :] = jnp.where(lane < after, strip, 0.0) * scale
            end = top + LANES
            if after < end:
                update = gram(thirds(strip), columns)[after - top :, :]
                lane = lax.broadcasted_iota(jnp.int32, (end - after, NB), 1)
                below = jnp.where((lane >= first) & (lane < after), 0.0, work[after:end, :])
                work[after:end, :] = below - update
            if between is not None:
                between(first // STRIP)
            strips.append(strip)
        if top + LANES < NB:
            upper = jnp.concatenate(strips, axis=0)
            lane = lax.broadcasted_iota(jnp.int32, (LANES, NB), 1)
            row = lax.broadcasted_iota(jnp.int32, (LANES, NB), 0) + top
            upper = jnp.where((lane > row) & (lane < top + LANES), 0.0, upper)
            update = gram(thirds(upper), slice(top + LANES, top + 2 * LANES))
            below = jnp.where(lane < top + LANES, 0.0, work[top + LANES :, :])
            work[top + LANES :, :] = below - update


def block_of(shares):
    return shares.reshape((NB, NB))


def first_kernel(mixed, inverse):
    block = block_of(mixed[:, :PART])
    row, column = scales(diagonal_of(block))
    inverse[...] = block * row * column
    invert_factor(inverse, row)


def second_kernel(
    row_index, inverse0, mixed, rest, own, prev, factor, trailing,
    work, before, middle, left, right, tail, arrive, leave,
):
    fetch = pltpu.make_async_copy(prev, before, arrive)
    fetch.start()
    x0 = inverse0[...]
    strip_row = lax.broadcasted_iota(jnp.int32, (NB, NB), 0) // STRIP
    strip_col = lax.broadcasted_iota(jnp.int32, (NB, NB), 1) // STRIP
    diagonal = mixed[: STRIP // SUB, PART:].reshape((STRIP, NB))
    diagonal = jnp.concatenate([diagonal] * (NB // STRIP), axis=0)
    block = jnp.where(strip_row < strip_col, block_of(mixed[:, :PART]).T, diagonal)
    w1 = dot(x0, block_of(rest[:, 0]), (1, 0))
    scale, column = scales(diagonal_of(diagonal) - jnp.sum(w1 * w1, axis=0, keepdims=True))
    reduced = block[:LANES] - dot(w1[:, :LANES], w1, (0, 0))
    work[:LANES, :] = reduced * scale * column[:LANES]
    w2 = dot(x0, block_of(rest[:, 1]), (1, 1))
    cross = block_of(rest[:, 2]) - dot(w2, w1, (0, 0))
    rows_here = own.shape[0]
    steps = LANES // STRIP
    piece = rows_here // steps
    row = row_index[0] * rows_here + lax.broadcasted_iota(jnp.int32, (rows_here, NB), 0)
    window = []
    writes = [
        pltpu.make_async_copy(left, factor.at[:, pl.ds(0, NB)], leave.at[0]),
        pltpu.make_async_copy(right, factor.at[:, pl.ds(NB, NB)], leave.at[1]),
        pltpu.make_async_copy(tail, trailing, leave.at[2]),
    ]

    def between(s):
        at = pl.ds(s % steps * piece, piece)
        if s == 0:
            reduced = block[LANES:] - dot(w1[:, LANES:], w1, (0, 0))
            work[LANES:, :] = reduced * scale * column[LANES:]
            fetch.wait()
        if s < steps:
            lower = dot(own[at, :NB] - before[at, :NB], x0, (1, 1))
            left[at, :] = lower
            middle[at, :] = own[at, NB:PANELW] - before[at, NB:PANELW] - dot(lower, w1, (1, 0))
            tail[at, :] = own[at, PANELW:] - before[at, PANELW:] - dot(lower, w2, (1, 0))
            return
        if s == steps:
            writes[0].start()
            window.append(dot(work[:LANES, :LANES], cross[:, :LANES], (1, 1)))
        lower = dot(middle[at, :LANES], work[:LANES, :LANES], (1, 1))
        right[at, :LANES] = jnp.where(row[s % steps * piece :][:piece, :LANES] >= NB, lower, 0.0)
        tail[at, :] = tail[at, :] - dot(lower, window[0], (1, 0))

    invert_factor(work, scale, between)
    x1 = work[LANES:, :]
    window.append(dot(x1, cross, (1, 1)))
    lower = dot(middle[...], x1, (1, 1))
    right[:, LANES:] = jnp.where(row[:, :LANES] >= NB, lower, 0.0)
    writes[1].start()
    tail[...] = jnp.where(row >= PANELW, tail[...] - dot(lower, window[1], (1, 0)), 0.0)
    writes[2].start()
    for write in writes:
        write.wait()


def exchange(blocks):
    return lax.all_to_all(blocks, "row", 0, 0, tiled=True)


def head_shares(block, row_index, count):
    first, second = block[:NB, :NB], block[NB:PANELW, NB:PANELW]
    strip_row = jnp.arange(NB)[:, None] // STRIP
    strip_col = jnp.arange(NB)[None, :] // STRIP
    mixed = jnp.where((strip_row <= strip_col) | (row_index == 1), first, second)
    strips = second.reshape(NB // STRIP, STRIP, NB)
    own_strip = jnp.arange(NB // STRIP)[:, None, None] == strip_col[None]
    diagonal = jnp.sum(jnp.where(own_strip, strips, 0.0), axis=0).reshape(-1, SUB, NB)
    diagonal = jnp.pad(diagonal, ((0, count - diagonal.shape[0]), (0, 0), (0, 0)))
    parts = [mixed.reshape(count, PART, NB), diagonal, block[:NB, NB:PANELW].reshape(count, PART, NB)]
    return jnp.concatenate(parts, axis=1)


def copies(share, count):
    return jnp.broadcast_to(share[None], (count,) + share.shape)


def per_device(schur_own, outgoing):
    own = schur_own[0]
    out = outgoing[0]
    rows_here = own.shape[0]
    count = lax.axis_size("row")
    row_index = lax.axis_index("row").astype(jnp.int32)
    pairs = [(s, s + 1) for s in range(lax.axis_size("slab") - 1)]
    vmem = pl.BlockSpec(memory_space=pltpu.VMEM)
    smem = pl.BlockSpec(memory_space=pltpu.SMEM)
    params = pltpu.CompilerParams(vmem_limit_bytes=VMEM_BYTES)

    sent = head_shares(out, row_index, count)
    holders = [(s * count + r, t * count + r) for s, t in pairs for r in range(2)]
    came = lax.ppermute(sent, ("slab", "row"), holders)
    own, _ = lax.optimization_barrier((own, sent))
    kept = head_shares(own, row_index, count)
    out, _ = lax.optimization_barrier((out, kept))
    prev = lax.ppermute(out, "slab", pairs)
    shares = exchange(kept - came)[:2]
    mixed = exchange(copies(shares[0, : PART + SUB], count))
    rest = jnp.stack([shares[0, PART + SUB :], shares[1, :PART], shares[1, PART + SUB :]])
    rest, mixed = lax.optimization_barrier((copies(rest, count), mixed))
    rest = exchange(rest)

    inverse0 = pl.pallas_call(
        first_kernel,
        out_shape=jax.ShapeDtypeStruct((NB, NB), jnp.float32),
        in_specs=[vmem],
        out_specs=vmem,
        compiler_params=params,
        cost_estimate=pl.CostEstimate(
            flops=400 * NB**3, bytes_accessed=8 * NB**2, transcendentals=NB),
        name="panel_inverse",
    )(mixed)

    factor, trailing = pl.pallas_call(
        second_kernel,
        out_shape=(
            jax.ShapeDtypeStruct((rows_here, PANELW), jnp.float32),
            jax.ShapeDtypeStruct((rows_here, COLS - PANELW), jnp.float32),
        ),
        in_specs=[smem] + [vmem] * 4 + [pl.BlockSpec(memory_space=pl.ANY)],
        out_specs=(pl.BlockSpec(memory_space=pl.ANY), pl.BlockSpec(memory_space=pl.ANY)),
        scratch_shapes=[
            pltpu.VMEM((NB, NB), jnp.float32),
            pltpu.VMEM((rows_here, COLS), jnp.float32),
        ]
        + [pltpu.VMEM((rows_here, NB), jnp.float32)] * 4
        + [pltpu.SemaphoreType.DMA, pltpu.SemaphoreType.DMA((3,))],
        compiler_params=params,
        name="panel_update",
    )(row_index[None], inverse0, mixed, rest, own, prev)
    return factor[None], trailing[None]


def solution(mesh):
    specs = (P("slab", "row", None), P("slab", "row", None))
    return jax.shard_map(
        per_device, mesh=mesh, in_specs=specs, out_specs=specs, check_vma=False
    )
```

```python
import jax
import jax.numpy as jnp
from jax import lax
from jax.experimental import pallas as pl
from jax.experimental.pallas import tpu as pltpu
from jax.sharding import PartitionSpec as P

NB = 256
PANELW = 512
COLS = 768
PART = 16
HALVES = 2 * PART
STRIP = 32
SUB = 8
LANES = 128
VMEM_BYTES = 48 * 1024 * 1024


def dot(a, b, contract):
    return lax.dot_general(
        a, b, ((contract[:1], contract[1:]), ((), ())),
        precision=lax.Precision.HIGHEST, preferred_element_type=jnp.float32,
    )


def eliminate_strip(rows, first):
    groups = len(rows)
    lane = lax.broadcasted_iota(jnp.int32, (SUB, NB), 1)
    sub = lax.broadcasted_iota(jnp.int32, (SUB, NB), 0)
    for t in range(groups):
        col = first + SUB * t
        in_block = (lane >= col) & (lane < col + SUB)
        columns = [
            [jnp.broadcast_to(rows[g][:, col + j : col + j + 1], (SUB, LANES)) for j in range(SUB)]
            for g in range(t, groups)
        ]
        a = [
            [jnp.broadcast_to(columns[0][k][i : i + 1, :], (SUB, LANES)) if i >= k else None
             for k in range(SUB)]
            for i in range(SUB)
        ]
        start = jnp.where(in_block, (lane == col + sub).astype(jnp.float32), rows[t])
        u = [jnp.broadcast_to(start[i : i + 1, :], (SUB, NB)) for i in range(SUB)]
        inv = [None] * SUB
        low = [[None] * SUB for _ in range(SUB)]
        for j in range(0, SUB, 4):
            p, q, r = a[j][j], a[j + 1][j], a[j + 1][j + 1]
            det = p * r - q * q
            left = {m: r * a[m][j] - q * a[m][j + 1] for m in (j + 2, j + 3)}
            right = {m: p * a[m][j + 1] - q * a[m][j] for m in (j + 2, j + 3)}
            scaled = lambda m, n: det * a[m][n] - (a[n][j] * left[m] + a[n][j + 1] * right[m])
            third = scaled(j + 2, j + 2)
            cross = scaled(j + 3, j + 2)
            both = third * scaled(j + 3, j + 3) - cross * cross
            inv[j] = lax.rsqrt(p)
            root, root_third = lax.rsqrt(det), lax.rsqrt(third)
            inv[j + 1] = (p * inv[j]) * root
            inv[j + 2] = (det * root) * root_third
            inv[j + 3] = ((det * root) * (third * root_third)) * lax.rsqrt(both)
            for c in range(j, j + 4):
                for k in range(c + 1, SUB):
                    value = a[k][c]
                    for e in range(j, c):
                        value = value - low[k][e] * low[c][e]
                    low[k][c] = value * inv[c]
            for k in range(j + 4, SUB):
                for m in range(j + 4, k + 1):
                    for c in range(j, j + 4):
                        a[k][m] = a[k][m] - low[k][c] * low[m][c]
        wide = lambda x: jnp.concatenate([x, x], axis=1)
        for j in range(SUB):
            u[j] = u[j] * wide(inv[j])
            for k in range(j + 1, SUB):
                u[k] = u[k] - wide(low[k][j]) * u[j]
        packed = u[0]
        for j in range(1, SUB):
            packed = jnp.where(sub == j, u[j], packed)
        rows[t] = packed
        for g in range(t + 1, groups):
            col_g = columns[g - t]
            total = jnp.where(in_block, 0.0, rows[g])
            for j in range(SUB):
                col_g[j] = col_g[j] * inv[j]
                for k in range(j + 1, SUB):
                    col_g[k] = col_g[k] - col_g[j] * low[k][j]
                total = total - wide(col_g[j]) * u[j]
            rows[g] = total
    return rows


def thirds(x):
    high = x.astype(jnp.bfloat16)
    rest = x - high.astype(jnp.float32)
    middle = rest.astype(jnp.bfloat16)
    return high, middle, (rest - middle.astype(jnp.float32)).astype(jnp.bfloat16)


def gram(parts, columns):
    high, middle, low = parts
    left = jnp.concatenate([x[:, columns] for x in (high, high, middle, high, low, middle)], axis=0)
    right = jnp.concatenate([high, middle, high, low, high, middle], axis=0)
    return lax.dot_general(
        left, right, (((0,), (0,)), ((), ())), preferred_element_type=jnp.float32
    )


def scales(diagonal):
    row = lax.rsqrt(diagonal)
    on_diagonal = lax.broadcasted_iota(jnp.int32, (NB, NB), 0) == lax.broadcasted_iota(
        jnp.int32, (NB, NB), 1)
    return row, jnp.sum(jnp.where(on_diagonal, row, 0.0), axis=1, keepdims=True)


def diagonal_of(block):
    on_diagonal = lax.broadcasted_iota(jnp.int32, (NB, NB), 0) == lax.broadcasted_iota(
        jnp.int32, (NB, NB), 1)
    return jnp.sum(jnp.where(on_diagonal, block, 0.0), axis=0, keepdims=True)


def invert_factor(work, scale, between=None):
    groups = STRIP // SUB
    for half in range(NB // LANES):
        top = half * LANES
        columns = slice(top, top + LANES)
        strips = []
        for s in range(LANES // STRIP):
            first = top + STRIP * s
            after = first + STRIP
            rows = [work[first + SUB * g : first + SUB * (g + 1), :] for g in range(groups)]
            rows = eliminate_strip(rows, first)
            strip = jnp.concatenate(rows, axis=0)
            lane = lax.broadcasted_iota(jnp.int32, (STRIP, NB), 1)
            row = lax.broadcasted_iota(jnp.int32, (STRIP, NB), 0) + first
            strip = jnp.where((lane > row) & (lane < after), 0.0, strip)
            work[first:after, :] = jnp.where(lane < after, strip, 0.0) * scale
            end = top + LANES
            if after < end:
                update = gram(thirds(strip), columns)[after - top :, :]
                lane = lax.broadcasted_iota(jnp.int32, (end - after, NB), 1)
                below = jnp.where((lane >= first) & (lane < after), 0.0, work[after:end, :])
                work[after:end, :] = below - update
            if between is not None:
                between(first // STRIP)
            strips.append(strip)
        if top + LANES < NB:
            upper = jnp.concatenate(strips, axis=0)
            lane = lax.broadcasted_iota(jnp.int32, (LANES, NB), 1)
            row = lax.broadcasted_iota(jnp.int32, (LANES, NB), 0) + top
            upper = jnp.where((lane > row) & (lane < top + LANES), 0.0, upper)
            update = gram(thirds(upper), slice(top + LANES, top + 2 * LANES))
            below = jnp.where(lane < top + LANES, 0.0, work[top + LANES :, :])
            work[top + LANES :, :] = below - update


def block_of(shares):
    left, right = shares[:, :PART].reshape((NB, LANES)), shares[:, PART:].reshape((NB, LANES))
    return jnp.concatenate([left, right], axis=1)


def first_kernel(mixed, inverse):
    block = block_of(mixed[:, :HALVES])
    row, column = scales(diagonal_of(block))
    inverse[...] = block * row * column
    invert_factor(inverse, row)


def second_kernel(
    row_index, inverse0, mixed, rest, own, prev, factor, trailing,
    work, before, middle, left, right, tail, arrive, leave,
):
    fetch = pltpu.make_async_copy(prev, before, arrive)
    fetch.start()
    x0 = inverse0[...]
    strip_row = lax.broadcasted_iota(jnp.int32, (NB, NB), 0) // STRIP
    strip_col = lax.broadcasted_iota(jnp.int32, (NB, NB), 1) // STRIP
    pieces = mixed[: 2 * STRIP // SUB, HALVES:].reshape((2 * STRIP, LANES))
    diagonal = jnp.concatenate([pieces[:STRIP], pieces[STRIP:]], axis=1)
    diagonal = jnp.concatenate([diagonal] * (NB // STRIP), axis=0)
    block = jnp.where(strip_row < strip_col, block_of(mixed[:, :HALVES]).T, diagonal)
    w1 = dot(x0, block_of(rest[:, 0]), (1, 0))
    scale, column = scales(diagonal_of(diagonal) - jnp.sum(w1 * w1, axis=0, keepdims=True))
    reduced = block[:LANES] - dot(w1[:, :LANES], w1, (0, 0))
    work[:LANES, :] = reduced * scale * column[:LANES]
    w2 = dot(x0, block_of(rest[:, 1]), (1, 1))
    cross = block_of(rest[:, 2]) - dot(w2, w1, (0, 0))
    rows_here = own.shape[0]
    steps = LANES // STRIP
    piece = rows_here // steps
    row = row_index[0] * rows_here + lax.broadcasted_iota(jnp.int32, (rows_here, NB), 0)
    window = []
    writes = [
        pltpu.make_async_copy(left, factor.at[:, pl.ds(0, NB)], leave.at[0]),
        pltpu.make_async_copy(right, factor.at[:, pl.ds(NB, NB)], leave.at[1]),
        pltpu.make_async_copy(tail, trailing, leave.at[2]),
    ]

    def between(s):
        at = pl.ds(s % steps * piece, piece)
        if s == 0:
            reduced = block[LANES:] - dot(w1[:, LANES:], w1, (0, 0))
            work[LANES:, :] = reduced * scale * column[LANES:]
            fetch.wait()
        if s < steps:
            lower = dot(own[at, :NB] - before[at, :NB], x0, (1, 1))
            left[at, :] = lower
            middle[at, :] = own[at, NB:PANELW] - before[at, NB:PANELW] - dot(lower, w1, (1, 0))
            tail[at, :] = own[at, PANELW:] - before[at, PANELW:] - dot(lower, w2, (1, 0))
            return
        if s == steps:
            writes[0].start()
            window.append(dot(work[:LANES, :LANES], cross[:, :LANES], (1, 1)))
        lower = dot(middle[at, :LANES], work[:LANES, :LANES], (1, 1))
        right[at, :LANES] = jnp.where(row[s % steps * piece :][:piece, :LANES] >= NB, lower, 0.0)
        tail[at, :] = tail[at, :] - dot(lower, window[0], (1, 0))

    invert_factor(work, scale, between)
    x1 = work[LANES:, :]
    window.append(dot(x1, cross, (1, 1)))
    lower = dot(middle[...], x1, (1, 1))
    right[:, LANES:] = jnp.where(row[:, :LANES] >= NB, lower, 0.0)
    writes[1].start()
    tail[...] = jnp.where(row >= PANELW, tail[...] - dot(lower, window[1], (1, 0)), 0.0)
    writes[2].start()
    for write in writes:
        write.wait()


def exchange(blocks):
    return lax.all_to_all(blocks, "row", 0, 0, tiled=True)


def share_kernel(row_index, block, shares):
    strip_row = lax.broadcasted_iota(jnp.int32, (NB, NB), 0) // STRIP
    strip_col = lax.broadcasted_iota(jnp.int32, (NB, NB), 1) // STRIP
    upper = (strip_row <= strip_col) | (row_index[0] == 1)
    mixed = jnp.where(upper, block[:NB, :NB], block[NB:, NB:])
    strip = lax.broadcasted_iota(jnp.int32, (STRIP, NB), 1) // STRIP
    diagonal = jnp.zeros((STRIP, NB), jnp.float32)
    for i in range(NB // STRIP):
        rows = block[NB + STRIP * i : NB + STRIP * (i + 1), NB:]
        diagonal = jnp.where(strip == i, rows, diagonal)
    count = shares.shape[0]
    pieces = STRIP // SUB
    half = lambda x, i: x[:, i * LANES : (i + 1) * LANES]
    shares[2 * pieces :, HALVES : HALVES + SUB] = jnp.zeros(
        (count - 2 * pieces, SUB, LANES), jnp.float32)
    for i in range(2):
        shares[i * pieces : (i + 1) * pieces, HALVES : HALVES + SUB] = half(diagonal, i).reshape(
            (pieces, SUB, LANES))
        shares[:, i * PART : (i + 1) * PART] = half(mixed, i).reshape((count, PART, LANES))
        at = HALVES + SUB + i * PART
        shares[:, at : at + PART] = half(block[:NB, NB:], i).reshape((count, PART, LANES))


def head_shares(block, row_index, count):
    shape = (count, 2 * HALVES + SUB, LANES)
    return pl.pallas_call(
        share_kernel,
        grid=(1,),
        out_shape=jax.ShapeDtypeStruct(shape, jnp.float32),
        in_specs=[
            pl.BlockSpec(memory_space=pltpu.SMEM),
            pl.BlockSpec((PANELW, PANELW), lambda i: (0, 0)),
        ],
        out_specs=pl.BlockSpec(shape, lambda i: (0, 0, 0)),
        compiler_params=pltpu.CompilerParams(vmem_limit_bytes=VMEM_BYTES),
        name="head_shares",
    )(row_index[None], block)


def copies(share, count):
    return jnp.broadcast_to(share[None], (count,) + share.shape)


def per_device(schur_own, outgoing):
    own = schur_own[0]
    out = outgoing[0]
    rows_here = own.shape[0]
    count = lax.axis_size("row")
    row_index = lax.axis_index("row").astype(jnp.int32)
    pairs = [(s, s + 1) for s in range(lax.axis_size("slab") - 1)]
    vmem = pl.BlockSpec(memory_space=pltpu.VMEM)
    smem = pl.BlockSpec(memory_space=pltpu.SMEM)
    params = pltpu.CompilerParams(vmem_limit_bytes=VMEM_BYTES)

    sent = head_shares(out, row_index, count)
    holders = [(s * count + r, t * count + r) for s, t in pairs for r in range(2)]
    came = lax.ppermute(sent, ("slab", "row"), holders)
    own, _ = lax.optimization_barrier((own, sent))
    kept = head_shares(own, row_index, count)
    out, _ = lax.optimization_barrier((out, kept))
    prev = lax.ppermute(out, "slab", pairs)
    shares = exchange(kept - came)[:2]
    mixed = exchange(copies(shares[0, : HALVES + SUB], count))
    rest = jnp.stack([shares[0, HALVES + SUB :], shares[1, :HALVES], shares[1, HALVES + SUB :]])
    rest, mixed = lax.optimization_barrier((copies(rest, count), mixed))
    rest = exchange(rest)

    inverse0 = pl.pallas_call(
        first_kernel,
        out_shape=jax.ShapeDtypeStruct((NB, NB), jnp.float32),
        in_specs=[vmem],
        out_specs=vmem,
        compiler_params=params,
        cost_estimate=pl.CostEstimate(
            flops=400 * NB**3, bytes_accessed=8 * NB**2, transcendentals=NB),
        name="panel_inverse",
    )(mixed)

    factor, trailing = pl.pallas_call(
        second_kernel,
        out_shape=(
            jax.ShapeDtypeStruct((rows_here, PANELW), jnp.float32),
            jax.ShapeDtypeStruct((rows_here, COLS - PANELW), jnp.float32),
        ),
        in_specs=[smem] + [vmem] * 4 + [pl.BlockSpec(memory_space=pl.ANY)],
        out_specs=(pl.BlockSpec(memory_space=pl.ANY), pl.BlockSpec(memory_space=pl.ANY)),
        scratch_shapes=[
            pltpu.VMEM((NB, NB), jnp.float32),
            pltpu.VMEM((rows_here, COLS), jnp.float32),
        ]
        + [pltpu.VMEM((rows_here, NB), jnp.float32)] * 4
        + [pltpu.SemaphoreType.DMA, pltpu.SemaphoreType.DMA((3,))],
        compiler_params=params,
        name="panel_update",
    )(row_index[None], inverse0, mixed, rest, own, prev)
    return factor[None], trailing[None]


def solution(mesh):
    specs = (P("slab", "row", None), P("slab", "row", None))
    return jax.shard_map(
        per_device, mesh=mesh, in_specs=specs, out_specs=specs, check_vma=False
    )
```

```python
import jax
import jax.numpy as jnp
from jax import lax
from jax.experimental import pallas as pl
from jax.experimental.pallas import tpu as pltpu
from jax.sharding import PartitionSpec as P

NB = 256
PANELW = 512
COLS = 768
PART = 16
HALVES = 2 * PART
STRIP = 32
SUB = 8
LANES = 128
VMEM_BYTES = 48 * 1024 * 1024


def dot(a, b, contract):
    return lax.dot_general(
        a, b, ((contract[:1], contract[1:]), ((), ())),
        precision=lax.Precision.HIGHEST, preferred_element_type=jnp.float32,
    )


def eliminate_strip(rows, first):
    groups = len(rows)
    lane = lax.broadcasted_iota(jnp.int32, (SUB, NB), 1)
    sub = lax.broadcasted_iota(jnp.int32, (SUB, NB), 0)
    for t in range(groups):
        col = first + SUB * t
        in_block = (lane >= col) & (lane < col + SUB)
        columns = [
            [jnp.broadcast_to(rows[g][:, col + j : col + j + 1], (SUB, LANES)) for j in range(SUB)]
            for g in range(t, groups)
        ]
        a = [
            [jnp.broadcast_to(columns[0][k][i : i + 1, :], (SUB, LANES)) if i >= k else None
             for k in range(SUB)]
            for i in range(SUB)
        ]
        start = jnp.where(in_block, (lane == col + sub).astype(jnp.float32), rows[t])
        u = [jnp.broadcast_to(start[i : i + 1, :], (SUB, NB)) for i in range(SUB)]
        inv = [None] * SUB
        low = [[None] * SUB for _ in range(SUB)]
        for j in range(0, SUB, 4):
            p, q, r = a[j][j], a[j + 1][j], a[j + 1][j + 1]
            det = p * r - q * q
            left = {m: r * a[m][j] - q * a[m][j + 1] for m in (j + 2, j + 3)}
            right = {m: p * a[m][j + 1] - q * a[m][j] for m in (j + 2, j + 3)}
            scaled = lambda m, n: det * a[m][n] - (a[n][j] * left[m] + a[n][j + 1] * right[m])
            third = scaled(j + 2, j + 2)
            cross = scaled(j + 3, j + 2)
            both = third * scaled(j + 3, j + 3) - cross * cross
            inv[j] = lax.rsqrt(p)
            root, root_third = lax.rsqrt(det), lax.rsqrt(third)
            inv[j + 1] = (p * inv[j]) * root
            inv[j + 2] = (det * root) * root_third
            inv[j + 3] = ((det * root) * (third * root_third)) * lax.rsqrt(both)
            for c in range(j, j + 4):
                for k in range(c + 1, SUB):
                    value = a[k][c]
                    for e in range(j, c):
                        value = value - low[k][e] * low[c][e]
                    low[k][c] = value * inv[c]
            for k in range(j + 4, SUB):
                for m in range(j + 4, k + 1):
                    for c in range(j, j + 4):
                        a[k][m] = a[k][m] - low[k][c] * low[m][c]
        wide = lambda x: jnp.concatenate([x, x], axis=1)
        for j in range(SUB):
            u[j] = u[j] * wide(inv[j])
            for k in range(j + 1, SUB):
                u[k] = u[k] - wide(low[k][j]) * u[j]
        packed = u[0]
        for j in range(1, SUB):
            packed = jnp.where(sub == j, u[j], packed)
        rows[t] = packed
        for g in range(t + 1, groups):
            col_g = columns[g - t]
            total = jnp.where(in_block, 0.0, rows[g])
            for j in range(SUB):
                col_g[j] = col_g[j] * inv[j]
                for k in range(j + 1, SUB):
                    col_g[k] = col_g[k] - col_g[j] * low[k][j]
                total = total - wide(col_g[j]) * u[j]
            rows[g] = total
    return rows


def halves(x):
    high = x.astype(jnp.bfloat16)
    return high, (x - high.astype(jnp.float32)).astype(jnp.bfloat16)


def dot_halves(a, b, contract):
    product = lambda x, y: lax.dot_general(
        x, y, ((contract[:1], contract[1:]), ((), ())), preferred_element_type=jnp.float32)
    return product(a[0], b[0]) + (product(a[0], b[1]) + product(a[1], b[0]))


def thirds(x):
    high = x.astype(jnp.bfloat16)
    rest = x - high.astype(jnp.float32)
    middle = rest.astype(jnp.bfloat16)
    return high, middle, (rest - middle.astype(jnp.float32)).astype(jnp.bfloat16)


def gram(parts, columns):
    high, middle, low = parts
    left = jnp.concatenate([x[:, columns] for x in (high, high, middle, high, low, middle)], axis=0)
    right = jnp.concatenate([high, middle, high, low, high, middle], axis=0)
    return lax.dot_general(
        left, right, (((0,), (0,)), ((), ())), preferred_element_type=jnp.float32
    )


def scales(diagonal):
    row = lax.rsqrt(diagonal)
    on_diagonal = lax.broadcasted_iota(jnp.int32, (NB, NB), 0) == lax.broadcasted_iota(
        jnp.int32, (NB, NB), 1)
    return row, jnp.sum(jnp.where(on_diagonal, row, 0.0), axis=1, keepdims=True)


def diagonal_of(block):
    on_diagonal = lax.broadcasted_iota(jnp.int32, (NB, NB), 0) == lax.broadcasted_iota(
        jnp.int32, (NB, NB), 1)
    return jnp.sum(jnp.where(on_diagonal, block, 0.0), axis=0, keepdims=True)


def invert_factor(work, scale, between=None):
    groups = STRIP // SUB
    for half in range(NB // LANES):
        top = half * LANES
        columns = slice(top, top + LANES)
        strips = []
        for s in range(LANES // STRIP):
            first = top + STRIP * s
            after = first + STRIP
            rows = [work[first + SUB * g : first + SUB * (g + 1), :] for g in range(groups)]
            rows = eliminate_strip(rows, first)
            strip = jnp.concatenate(rows, axis=0)
            lane = lax.broadcasted_iota(jnp.int32, (STRIP, NB), 1)
            row = lax.broadcasted_iota(jnp.int32, (STRIP, NB), 0) + first
            strip = jnp.where((lane > row) & (lane < after), 0.0, strip)
            work[first:after, :] = jnp.where(lane < after, strip, 0.0) * scale
            end = top + LANES
            if after < end:
                update = gram(thirds(strip), columns)[after - top :, :]
                lane = lax.broadcasted_iota(jnp.int32, (end - after, NB), 1)
                below = jnp.where((lane >= first) & (lane < after), 0.0, work[after:end, :])
                work[after:end, :] = below - update
            if between is not None:
                between(first // STRIP)
            strips.append(strip)
        if top + LANES < NB:
            upper = jnp.concatenate(strips, axis=0)
            lane = lax.broadcasted_iota(jnp.int32, (LANES, NB), 1)
            row = lax.broadcasted_iota(jnp.int32, (LANES, NB), 0) + top
            upper = jnp.where((lane > row) & (lane < top + LANES), 0.0, upper)
            update = gram(thirds(upper), slice(top + LANES, top + 2 * LANES))
            below = jnp.where(lane < top + LANES, 0.0, work[top + LANES :, :])
            work[top + LANES :, :] = below - update


def block_of(shares):
    left, right = shares[:, :PART].reshape((NB, LANES)), shares[:, PART:].reshape((NB, LANES))
    return jnp.concatenate([left, right], axis=1)


def first_kernel(mixed, inverse):
    block = block_of(mixed[:, :HALVES])
    row, column = scales(diagonal_of(block))
    inverse[...] = block * row * column
    invert_factor(inverse, row)


def second_kernel(
    row_index, inverse0, mixed, rest, own, prev, factor, trailing,
    work, before, middle, left, right, tail, arrive, leave,
):
    fetch = pltpu.make_async_copy(prev, before, arrive)
    fetch.start()
    x0 = inverse0[...]
    strip_row = lax.broadcasted_iota(jnp.int32, (NB, NB), 0) // STRIP
    strip_col = lax.broadcasted_iota(jnp.int32, (NB, NB), 1) // STRIP
    pieces = mixed[: 2 * STRIP // SUB, HALVES:].reshape((2 * STRIP, LANES))
    diagonal = jnp.concatenate([pieces[:STRIP], pieces[STRIP:]], axis=1)
    diagonal = jnp.concatenate([diagonal] * (NB // STRIP), axis=0)
    block = jnp.where(strip_row < strip_col, block_of(mixed[:, :HALVES]).T, diagonal)
    w1 = dot(x0, block_of(rest[:, 0]), (1, 0))
    scale, column = scales(diagonal_of(diagonal) - jnp.sum(w1 * w1, axis=0, keepdims=True))
    reduced = block[:LANES] - dot(w1[:, :LANES], w1, (0, 0))
    work[:LANES, :] = reduced * scale * column[:LANES]
    w2 = dot(x0, block_of(rest[:, 1]), (1, 1))
    cross = block_of(rest[:, 2]) - dot(w2, w1, (0, 0))
    rows_here = own.shape[0]
    steps = LANES // STRIP
    piece = rows_here // steps
    row = row_index[0] * rows_here + lax.broadcasted_iota(jnp.int32, (rows_here, NB), 0)
    window = []
    writes = [
        pltpu.make_async_copy(left, factor.at[:, pl.ds(0, NB)], leave.at[0]),
        pltpu.make_async_copy(right, factor.at[:, pl.ds(NB, NB)], leave.at[1]),
        pltpu.make_async_copy(tail, trailing, leave.at[2]),
    ]

    w2_halves = halves(w2)

    def between(s):
        at = pl.ds(s % steps * piece, piece)
        if s == 0:
            reduced = block[LANES:] - dot(w1[:, LANES:], w1, (0, 0))
            work[LANES:, :] = reduced * scale * column[LANES:]
            fetch.wait()
        if s < steps:
            lower = dot(own[at, :NB] - before[at, :NB], x0, (1, 1))
            left[at, :] = lower
            middle[at, :] = own[at, NB:PANELW] - before[at, NB:PANELW] - dot(lower, w1, (1, 0))
            update = dot_halves(halves(lower), w2_halves, (1, 0))
            tail[at, :] = own[at, PANELW:] - before[at, PANELW:] - update
            return
        if s == steps:
            writes[0].start()
            window.append(halves(dot(work[:LANES, :LANES], cross[:, :LANES], (1, 1))))
        lower = dot(middle[at, :LANES], work[:LANES, :LANES], (1, 1))
        right[at, :LANES] = jnp.where(row[s % steps * piece :][:piece, :LANES] >= NB, lower, 0.0)
        tail[at, :] = tail[at, :] - dot_halves(halves(lower), window[0], (1, 0))

    invert_factor(work, scale, between)
    x1 = work[LANES:, :]
    window.append(halves(dot(x1, cross, (1, 1))))
    lower = dot(middle[...], x1, (1, 1))
    right[:, LANES:] = jnp.where(row[:, :LANES] >= NB, lower, 0.0)
    writes[1].start()
    total = tail[...] - dot_halves(halves(lower), window[1], (1, 0))
    tail[...] = jnp.where(row >= PANELW, total, 0.0)
    writes[2].start()
    for write in writes:
        write.wait()


def exchange(blocks):
    return lax.all_to_all(blocks, "row", 0, 0, tiled=True)


def share_kernel(row_index, block, shares):
    strip_row = lax.broadcasted_iota(jnp.int32, (NB, NB), 0) // STRIP
    strip_col = lax.broadcasted_iota(jnp.int32, (NB, NB), 1) // STRIP
    upper = (strip_row <= strip_col) | (row_index[0] == 1)
    mixed = jnp.where(upper, block[:NB, :NB], block[NB:, NB:])
    strip = lax.broadcasted_iota(jnp.int32, (STRIP, NB), 1) // STRIP
    diagonal = jnp.zeros((STRIP, NB), jnp.float32)
    for i in range(NB // STRIP):
        rows = block[NB + STRIP * i : NB + STRIP * (i + 1), NB:]
        diagonal = jnp.where(strip == i, rows, diagonal)
    count = shares.shape[0]
    pieces = STRIP // SUB
    half = lambda x, i: x[:, i * LANES : (i + 1) * LANES]
    shares[2 * pieces :, HALVES : HALVES + SUB] = jnp.zeros(
        (count - 2 * pieces, SUB, LANES), jnp.float32)
    for i in range(2):
        shares[i * pieces : (i + 1) * pieces, HALVES : HALVES + SUB] = half(diagonal, i).reshape(
            (pieces, SUB, LANES))
        shares[:, i * PART : (i + 1) * PART] = half(mixed, i).reshape((count, PART, LANES))
        at = HALVES + SUB + i * PART
        shares[:, at : at + PART] = half(block[:NB, NB:], i).reshape((count, PART, LANES))


def head_shares(block, row_index, count):
    shape = (count, 2 * HALVES + SUB, LANES)
    return pl.pallas_call(
        share_kernel,
        grid=(1,),
        out_shape=jax.ShapeDtypeStruct(shape, jnp.float32),
        in_specs=[
            pl.BlockSpec(memory_space=pltpu.SMEM),
            pl.BlockSpec((PANELW, PANELW), lambda i: (0, 0)),
        ],
        out_specs=pl.BlockSpec(shape, lambda i: (0, 0, 0)),
        compiler_params=pltpu.CompilerParams(vmem_limit_bytes=VMEM_BYTES),
        name="head_shares",
    )(row_index[None], block)


def copies(share, count):
    return jnp.broadcast_to(share[None], (count,) + share.shape)


def per_device(schur_own, outgoing):
    own = schur_own[0]
    out = outgoing[0]
    rows_here = own.shape[0]
    count = lax.axis_size("row")
    row_index = lax.axis_index("row").astype(jnp.int32)
    pairs = [(s, s + 1) for s in range(lax.axis_size("slab") - 1)]
    vmem = pl.BlockSpec(memory_space=pltpu.VMEM)
    smem = pl.BlockSpec(memory_space=pltpu.SMEM)
    params = pltpu.CompilerParams(vmem_limit_bytes=VMEM_BYTES)

    sent = head_shares(out, row_index, count)
    holders = [(s * count + r, t * count + r) for s, t in pairs for r in range(2)]
    came = lax.ppermute(sent, ("slab", "row"), holders)
    own, _ = lax.optimization_barrier((own, sent))
    kept = head_shares(own, row_index, count)
    out, _ = lax.optimization_barrier((out, kept))
    prev = lax.ppermute(out, "slab", pairs)
    shares = exchange(kept - came)[:2]
    mixed = exchange(copies(shares[0, : HALVES + SUB], count))
    rest = jnp.stack([shares[0, HALVES + SUB :], shares[1, :HALVES], shares[1, HALVES + SUB :]])
    rest, mixed = lax.optimization_barrier((copies(rest, count), mixed))
    rest = exchange(rest)

    inverse0 = pl.pallas_call(
        first_kernel,
        out_shape=jax.ShapeDtypeStruct((NB, NB), jnp.float32),
        in_specs=[vmem],
        out_specs=vmem,
        compiler_params=params,
        cost_estimate=pl.CostEstimate(
            flops=400 * NB**3, bytes_accessed=8 * NB**2, transcendentals=NB),
        name="panel_inverse",
    )(mixed)

    factor, trailing = pl.pallas_call(
        second_kernel,
        out_shape=(
            jax.ShapeDtypeStruct((rows_here, PANELW), jnp.float32),
            jax.ShapeDtypeStruct((rows_here, COLS - PANELW), jnp.float32),
        ),
        in_specs=[smem] + [vmem] * 4 + [pl.BlockSpec(memory_space=pl.ANY)],
        out_specs=(pl.BlockSpec(memory_space=pl.ANY), pl.BlockSpec(memory_space=pl.ANY)),
        scratch_shapes=[
            pltpu.VMEM((NB, NB), jnp.float32),
            pltpu.VMEM((rows_here, COLS), jnp.float32),
        ]
        + [pltpu.VMEM((rows_here, NB), jnp.float32)] * 4
        + [pltpu.SemaphoreType.DMA, pltpu.SemaphoreType.DMA((3,))],
        compiler_params=params,
        name="panel_update",
    )(row_index[None], inverse0, mixed, rest, own, prev)
    return factor[None], trailing[None]


def solution(mesh):
    specs = (P("slab", "row", None), P("slab", "row", None))
    return jax.shard_map(
        per_device, mesh=mesh, in_specs=specs, out_specs=specs, check_vma=False
    )
```

```python
import jax
import jax.numpy as jnp
from jax import lax
from jax.experimental import pallas as pl
from jax.experimental.pallas import tpu as pltpu
from jax.sharding import PartitionSpec as P

NB = 256
PANELW = 512
COLS = 768
PART = 16
HALVES = 2 * PART
STRIP = 32
SUB = 8
LANES = 128
VMEM_BYTES = 48 * 1024 * 1024


def dot(a, b, contract):
    return lax.dot_general(
        a, b, ((contract[:1], contract[1:]), ((), ())),
        precision=lax.Precision.HIGHEST, preferred_element_type=jnp.float32,
    )


def eliminate_strip(rows, first):
    groups = len(rows)
    lane = lax.broadcasted_iota(jnp.int32, (SUB, NB), 1)
    sub = lax.broadcasted_iota(jnp.int32, (SUB, NB), 0)
    for t in range(groups):
        col = first + SUB * t
        in_block = (lane >= col) & (lane < col + SUB)
        columns = [
            [jnp.broadcast_to(rows[g][:, col + j : col + j + 1], (SUB, LANES)) for j in range(SUB)]
            for g in range(t, groups)
        ]
        a = [
            [jnp.broadcast_to(columns[0][k][i : i + 1, :], (SUB, LANES)) if i >= k else None
             for k in range(SUB)]
            for i in range(SUB)
        ]
        start = jnp.where(in_block, (lane == col + sub).astype(jnp.float32), rows[t])
        u = [jnp.broadcast_to(start[i : i + 1, :], (SUB, NB)) for i in range(SUB)]
        inv = [None] * SUB
        low = [[None] * SUB for _ in range(SUB)]
        for j in range(0, SUB, 4):
            p, q, r = a[j][j], a[j + 1][j], a[j + 1][j + 1]
            det = p * r - q * q
            left = {m: r * a[m][j] - q * a[m][j + 1] for m in (j + 2, j + 3)}
            right = {m: p * a[m][j + 1] - q * a[m][j] for m in (j + 2, j + 3)}
            scaled = lambda m, n: det * a[m][n] - (a[n][j] * left[m] + a[n][j + 1] * right[m])
            third = scaled(j + 2, j + 2)
            cross = scaled(j + 3, j + 2)
            both = third * scaled(j + 3, j + 3) - cross * cross
            inv[j] = lax.rsqrt(p)
            root, root_third = lax.rsqrt(det), lax.rsqrt(third)
            inv[j + 1] = (p * inv[j]) * root
            inv[j + 2] = (det * root) * root_third
            inv[j + 3] = ((det * root) * (third * root_third)) * lax.rsqrt(both)
            for c in range(j, j + 4):
                for k in range(c + 1, SUB):
                    value = a[k][c]
                    for e in range(j, c):
                        value = value - low[k][e] * low[c][e]
                    low[k][c] = value * inv[c]
            for k in range(j + 4, SUB):
                for m in range(j + 4, k + 1):
                    for c in range(j, j + 4):
                        a[k][m] = a[k][m] - low[k][c] * low[m][c]
        wide = lambda x: jnp.concatenate([x, x], axis=1)
        for j in range(SUB):
            u[j] = u[j] * wide(inv[j])
            for k in range(j + 1, SUB):
                u[k] = u[k] - wide(low[k][j]) * u[j]
        packed = u[0]
        for j in range(1, SUB):
            packed = jnp.where(sub == j, u[j], packed)
        rows[t] = packed
        for g in range(t + 1, groups):
            col_g = columns[g - t]
            total = jnp.where(in_block, 0.0, rows[g])
            for j in range(SUB):
                col_g[j] = col_g[j] * inv[j]
                for k in range(j + 1, SUB):
                    col_g[k] = col_g[k] - col_g[j] * low[k][j]
                total = total - wide(col_g[j]) * u[j]
            rows[g] = total
    return rows


def thirds(x):
    high = x.astype(jnp.bfloat16)
    rest = x - high.astype(jnp.float32)
    middle = rest.astype(jnp.bfloat16)
    return high, middle, (rest - middle.astype(jnp.float32)).astype(jnp.bfloat16)


def gram(parts, columns):
    high, middle, low = parts
    left = jnp.concatenate([x[:, columns] for x in (high, high, middle, high, low, middle)], axis=0)
    right = jnp.concatenate([high, middle, high, low, high, middle], axis=0)
    return lax.dot_general(
        left, right, (((0,), (0,)), ((), ())), preferred_element_type=jnp.float32
    )


def scales(diagonal):
    row = lax.rsqrt(diagonal)
    on_diagonal = lax.broadcasted_iota(jnp.int32, (NB, NB), 0) == lax.broadcasted_iota(
        jnp.int32, (NB, NB), 1)
    return row, jnp.sum(jnp.where(on_diagonal, row, 0.0), axis=1, keepdims=True)


def diagonal_of(block):
    on_diagonal = lax.broadcasted_iota(jnp.int32, (NB, NB), 0) == lax.broadcasted_iota(
        jnp.int32, (NB, NB), 1)
    return jnp.sum(jnp.where(on_diagonal, block, 0.0), axis=0, keepdims=True)


def invert_factor(work, scale, between=None):
    groups = STRIP // SUB
    for half in range(NB // LANES):
        top = half * LANES
        columns = slice(top, top + LANES)
        strips = []
        for s in range(LANES // STRIP):
            first = top + STRIP * s
            after = first + STRIP
            rows = [work[first + SUB * g : first + SUB * (g + 1), :] for g in range(groups)]
            rows = eliminate_strip(rows, first)
            strip = jnp.concatenate(rows, axis=0)
            lane = lax.broadcasted_iota(jnp.int32, (STRIP, NB), 1)
            row = lax.broadcasted_iota(jnp.int32, (STRIP, NB), 0) + first
            strip = jnp.where((lane > row) & (lane < after), 0.0, strip)
            work[first:after, :] = jnp.where(lane < after, strip, 0.0) * scale
            end = top + LANES
            if after < end:
                update = gram(thirds(strip), columns)[after - top :, :]
                lane = lax.broadcasted_iota(jnp.int32, (end - after, NB), 1)
                below = jnp.where((lane >= first) & (lane < after), 0.0, work[after:end, :])
                work[after:end, :] = below - update
            if between is not None:
                between(first // STRIP)
            strips.append(strip)
        if top + LANES < NB:
            upper = jnp.concatenate(strips, axis=0)
            lane = lax.broadcasted_iota(jnp.int32, (LANES, NB), 1)
            row = lax.broadcasted_iota(jnp.int32, (LANES, NB), 0) + top
            upper = jnp.where((lane > row) & (lane < top + LANES), 0.0, upper)
            update = gram(thirds(upper), slice(top + LANES, top + 2 * LANES))
            below = jnp.where(lane < top + LANES, 0.0, work[top + LANES :, :])
            work[top + LANES :, :] = below - update


def block_of(shares):
    left, right = shares[:, :PART].reshape((NB, LANES)), shares[:, PART:].reshape((NB, LANES))
    return jnp.concatenate([left, right], axis=1)


def first_kernel(mixed, inverse):
    block = block_of(mixed[:, :HALVES])
    row, column = scales(diagonal_of(block))
    inverse[...] = block * row * column
    invert_factor(inverse, row)


def second_kernel(
    row_index, inverse0, mixed, rest, own, prev, factor, trailing,
    work, before, middle, left, right, tail, arrive, leave,
):
    fetch = pltpu.make_async_copy(prev, before, arrive)
    fetch.start()
    x0 = inverse0[...]
    strip_row = lax.broadcasted_iota(jnp.int32, (NB, NB), 0) // STRIP
    strip_col = lax.broadcasted_iota(jnp.int32, (NB, NB), 1) // STRIP
    pieces = mixed[: 2 * STRIP // SUB, HALVES:].reshape((2 * STRIP, LANES))
    diagonal = jnp.concatenate([pieces[:STRIP], pieces[STRIP:]], axis=1)
    diagonal = jnp.concatenate([diagonal] * (NB // STRIP), axis=0)
    block = jnp.where(strip_row < strip_col, block_of(mixed[:, :HALVES]).T, diagonal)
    w1 = dot(x0, block_of(rest[:, 0]), (1, 0))
    scale, column = scales(diagonal_of(diagonal) - jnp.sum(w1 * w1, axis=0, keepdims=True))
    reduced = block[:LANES] - dot(w1[:, :LANES], w1, (0, 0))
    work[:LANES, :] = reduced * scale * column[:LANES]
    w2 = dot(x0, block_of(rest[:, 1]), (1, 1))
    cross = block_of(rest[:, 2]) - dot(w2, w1, (0, 0))
    rows_here = own.shape[0]
    steps = LANES // STRIP
    piece = rows_here // steps
    row = row_index[0] * rows_here + lax.broadcasted_iota(jnp.int32, (rows_here, NB), 0)
    window = []
    writes = [
        pltpu.make_async_copy(left, factor.at[:, pl.ds(0, NB)], leave.at[0]),
        pltpu.make_async_copy(right, factor.at[:, pl.ds(NB, NB)], leave.at[1]),
        pltpu.make_async_copy(tail, trailing, leave.at[2]),
    ]

    def between(s):
        at = pl.ds(s % steps * piece, piece)
        if s == 0:
            reduced = block[LANES:] - dot(w1[:, LANES:], w1, (0, 0))
            work[LANES:, :] = reduced * scale * column[LANES:]
            fetch.wait()
        if s < steps:
            lower = dot(own[at, :NB] - before[at, :NB], x0, (1, 1))
            left[at, :] = lower
            middle[at, :] = own[at, NB:PANELW] - before[at, NB:PANELW] - dot(lower, w1, (1, 0))
            tail[at, :] = own[at, PANELW:] - before[at, PANELW:] - dot(lower, w2, (1, 0))
            return
        if s == steps:
            writes[0].start()
            window.append(dot(work[:LANES, :LANES], cross[:, :LANES], (1, 1)))
        lower = dot(middle[at, :LANES], work[:LANES, :LANES], (1, 1))
        right[at, :LANES] = jnp.where(row[s % steps * piece :][:piece, :LANES] >= NB, lower, 0.0)
        tail[at, :] = tail[at, :] - dot(lower, window[0], (1, 0))

    invert_factor(work, scale, between)
    x1 = work[LANES:, :]
    window.append(dot(x1, cross, (1, 1)))
    lower = dot(middle[...], x1, (1, 1))
    right[:, LANES:] = jnp.where(row[:, :LANES] >= NB, lower, 0.0)
    writes[1].start()
    tail[...] = jnp.where(row >= PANELW, tail[...] - dot(lower, window[1], (1, 0)), 0.0)
    writes[2].start()
    for write in writes:
        write.wait()


def exchange(blocks):
    return lax.all_to_all(blocks, "row", 0, 0, tiled=True)


def share_kernel(row_index, block, shares):
    strip_row = lax.broadcasted_iota(jnp.int32, (NB, NB), 0) // STRIP
    strip_col = lax.broadcasted_iota(jnp.int32, (NB, NB), 1) // STRIP
    upper = (strip_row <= strip_col) | (row_index[0] == 1)
    mixed = jnp.where(upper, block[:NB, :NB], block[NB:, NB:])
    strip = lax.broadcasted_iota(jnp.int32, (STRIP, NB), 1) // STRIP
    diagonal = jnp.zeros((STRIP, NB), jnp.float32)
    for i in range(NB // STRIP):
        rows = block[NB + STRIP * i : NB + STRIP * (i + 1), NB:]
        diagonal = jnp.where(strip == i, rows, diagonal)
    count = shares.shape[0]
    pieces = STRIP // SUB
    half = lambda x, i: x[:, i * LANES : (i + 1) * LANES]
    shares[2 * pieces :, HALVES : HALVES + SUB] = jnp.zeros(
        (count - 2 * pieces, SUB, LANES), jnp.float32)
    for i in range(2):
        shares[i * pieces : (i + 1) * pieces, HALVES : HALVES + SUB] = half(diagonal, i).reshape(
            (pieces, SUB, LANES))
        shares[:, i * PART : (i + 1) * PART] = half(mixed, i).reshape((count, PART, LANES))
        at = HALVES + SUB + i * PART
        shares[:, at : at + PART] = half(block[:NB, NB:], i).reshape((count, PART, LANES))


def head_shares(block, row_index, count):
    shape = (count, 2 * HALVES + SUB, LANES)
    return pl.pallas_call(
        share_kernel,
        grid=(1,),
        out_shape=jax.ShapeDtypeStruct(shape, jnp.float32),
        in_specs=[
            pl.BlockSpec(memory_space=pltpu.SMEM),
            pl.BlockSpec((PANELW, PANELW), lambda i: (0, 0)),
        ],
        out_specs=pl.BlockSpec(shape, lambda i: (0, 0, 0)),
        compiler_params=pltpu.CompilerParams(vmem_limit_bytes=VMEM_BYTES),
        name="head_shares",
    )(row_index[None], block)


def copies(share, count):
    return jnp.broadcast_to(share[None], (count,) + share.shape)


def per_device(schur_own, outgoing):
    own = schur_own[0]
    out = outgoing[0]
    rows_here = own.shape[0]
    count = lax.axis_size("row")
    row_index = lax.axis_index("row").astype(jnp.int32)
    pairs = [(s, s + 1) for s in range(lax.axis_size("slab") - 1)]
    vmem = pl.BlockSpec(memory_space=pltpu.VMEM)
    smem = pl.BlockSpec(memory_space=pltpu.SMEM)
    params = pltpu.CompilerParams(vmem_limit_bytes=VMEM_BYTES)

    sent = head_shares(out, row_index, count)
    holders = [(s * count + r, t * count + r) for s, t in pairs for r in range(2)]
    came = lax.ppermute(sent, ("slab", "row"), holders)
    own, _ = lax.optimization_barrier((own, sent))
    kept = head_shares(own, row_index, count)
    shares = exchange(kept - came)[:2]
    out, _ = lax.optimization_barrier((out, shares))
    prev = lax.ppermute(out, "slab", pairs)
    mixed = exchange(copies(shares[0, : HALVES + SUB], count))
    rest = jnp.stack([shares[0, HALVES + SUB :], shares[1, :HALVES], shares[1, HALVES + SUB :]])
    rest, mixed = lax.optimization_barrier((copies(rest, count), mixed))
    rest = exchange(rest)

    inverse0 = pl.pallas_call(
        first_kernel,
        out_shape=jax.ShapeDtypeStruct((NB, NB), jnp.float32),
        in_specs=[vmem],
        out_specs=vmem,
        compiler_params=params,
        cost_estimate=pl.CostEstimate(
            flops=400 * NB**3, bytes_accessed=8 * NB**2, transcendentals=NB),
        name="panel_inverse",
    )(mixed)

    factor, trailing = pl.pallas_call(
        second_kernel,
        out_shape=(
            jax.ShapeDtypeStruct((rows_here, PANELW), jnp.float32),
            jax.ShapeDtypeStruct((rows_here, COLS - PANELW), jnp.float32),
        ),
        in_specs=[smem] + [vmem] * 4 + [pl.BlockSpec(memory_space=pl.ANY)],
        out_specs=(pl.BlockSpec(memory_space=pl.ANY), pl.BlockSpec(memory_space=pl.ANY)),
        scratch_shapes=[
            pltpu.VMEM((NB, NB), jnp.float32),
            pltpu.VMEM((rows_here, COLS), jnp.float32),
        ]
        + [pltpu.VMEM((rows_here, NB), jnp.float32)] * 4
        + [pltpu.SemaphoreType.DMA, pltpu.SemaphoreType.DMA((3,))],
        compiler_params=params,
        name="panel_update",
    )(row_index[None], inverse0, mixed, rest, own, prev)
    return factor[None], trailing[None]


def solution(mesh):
    specs = (P("slab", "row", None), P("slab", "row", None))
    return jax.shard_map(
        per_device, mesh=mesh, in_specs=specs, out_specs=specs, check_vma=False
    )
```
